512 devices in a mesh: tm: 128 (over y_hi, z, x), height: 4 (over y_lo, core).
Axes of the slice: x: 4, y: 4 (y_hi: 2, y_lo: 2; y = y_hi * 2 + y_lo), z: 16, core: 2. Of those that a mesh axis runs over, the one named last changes fastest.
Arguments:
- frames_in: bfloat16 [512, 320, 512], P('tm', None, 'height'), may hold values from -6 to 6
- conv_spatial: bfloat16 [320, 2880], replicated, may hold values from -0.109375 to 0.109375
- conv_temporal: bfloat16 [320, 960], replicated, may hold values from -0.1875 to 0.1875
- w_query: bfloat16 [320, 320], replicated, may hold values from -2 to 2
- w_key: bfloat16 [320, 320], replicated, may hold values from -2 to 2
- w_value: bfloat16 [320, 320], replicated, may hold values from -0.3125 to 0.3125
- w_out: bfloat16 [320, 320], replicated, may hold values from -0.3125 to 0.3125
- win_left: int32 [5], replicated, may hold values from 0 to 8, as said below
- win_right: int32 [5], replicated, may hold values from 0 to 8, as said below
Outputs:
- frames_out: bfloat16 [512, 320, 512], P('tm', None, 'height')
The draws below stay inside these ranges and needn't reach their ends.
Inputs may be any that keep to these rules, and one draw needn't show every extreme that they name: `win_left`: some head reaches back exactly 8 frames. `win_right`: some head reaches ahead exactly 8 frames.
All inputs are finite; a program needn't handle non-finite values.
Results may differ from the reference program's by a relative error of at most 0.017.
Values may be sent and summed in bfloat16 or wider, within the bound.
A program may use at most 64 MiB of HBM per device.

```python
import math
import jax
import jax.numpy as jnp
from jax import lax

C = 320
HEADS = 5
HEAD_DIM = 64
F_DEV = 4
WIDE = 32
WMAX = 8
FRAMES = 512
ROWS = 16
CELLS = 512


def window_widths(key):
    widths = jax.random.randint(jax.random.fold_in(key, 1), (HEADS,), 0, WMAX + 1)
    chosen = jax.random.randint(jax.random.fold_in(key, 2), (), 0, HEADS)
    return jnp.where(jnp.arange(HEADS) == chosen, WMAX, widths).astype(jnp.int32)


def draw_win_left(key, part):
    key = jax.random.fold_in(key, 11)
    return window_widths(key)


def draw_win_right(key, part):
    key = jax.random.fold_in(key, 12)
    return window_widths(key)


def projection_draw(own_part):
    blended = own_part / math.sqrt(C)
    return jnp.clip(blended, -2.0, 2.0).astype(jnp.bfloat16)


def draw_w_query(key, part):
    key = jax.random.fold_in(key, 21)
    own_part = jax.random.normal(key, (C, C), jnp.float32)
    return projection_draw(own_part)


def draw_w_key(key, part):
    key = jax.random.fold_in(key, 22)
    own_part = jax.random.normal(key, (C, C), jnp.float32)
    return projection_draw(own_part)


def steps_of(own_key, dims, split, low, high):
    loudness = 1.0
    for dim, shards_of in split:
        steps = jax.random.uniform(jax.random.fold_in(jax.random.fold_in(own_key, 6), dim), (shards_of,), jnp.float32, low / len(split), high / len(split))
        loudness = loudness * jnp.repeat(jnp.exp(steps), dims[dim] // shards_of).reshape((-1,) + (1,) * (len(dims) - 1 - dim))
    return loudness


def scatter_about(rng, dims, width, bound, shards=(), kind=jnp.bfloat16):
    gain = steps_of(rng, dims, shards, -0.22, 0.18) if shards else 1.0
    entries = jax.random.normal(rng, dims, jnp.float32) * width * gain
    return jnp.minimum(jnp.maximum(entries, -bound), bound).astype(kind)


def setup_inputs(seed: int = 0) -> dict:
    key_list = jax.random.split(jax.random.key(seed), 10)
    return {
        "frames_in": scatter_about(key_list[0], (FRAMES, C, CELLS), 1.0, 6.0, ((0, 128), (2, 4))),
        "conv_spatial": scatter_about(key_list[1], (C, 9 * C), (9 * C) ** -0.5, 0.109375),
        "conv_temporal": scatter_about(key_list[2], (C, 3 * C), (3 * C) ** -0.5, 0.1875),
        "w_query": draw_w_query(jax.random.fold_in(key_list[9], 71), 0),
        "w_key": draw_w_key(jax.random.fold_in(key_list[9], 71), 0),
        "w_value": scatter_about(key_list[5], (C, C), C ** -0.5, 0.3125),
        "w_out": scatter_about(key_list[6], (C, C), C ** -0.5, 0.3125),
        "win_left": draw_win_left(jax.random.fold_in(key_list[9], 71), 0),
        "win_right": draw_win_right(jax.random.fold_in(key_list[9], 71), 0),
    }


def silu_round(source):
    widened = source.astype(jnp.float32)
    return jax.nn.silu(widened).astype(jnp.bfloat16)

def layer_norm(stream):
    widened = stream.astype(jnp.float32)
    centred = widened - lax.optimization_barrier(jnp.mean(widened, axis=1, keepdims=True))
    spread = lax.optimization_barrier(jnp.mean(centred * centred, axis=1, keepdims=True))
    return (centred * lax.rsqrt(spread + 1e-05)).astype(jnp.bfloat16)

def project(weight, source):
    return jnp.einsum('oi,fip->fop', weight.astype(jnp.float32), source.astype(jnp.float32)).astype(jnp.bfloat16)

def attend(queries, key_frames, value_frames, first_query, first_key, win_left, win_right, total_frames):
    query_count = queries.shape[0]
    key_count = key_frames.shape[0]
    cell_count = queries.shape[2]
    query_heads = queries.reshape(query_count, HEADS, HEAD_DIM, cell_count).astype(jnp.float32)
    key_heads = key_frames.reshape(key_count, HEADS, HEAD_DIM, cell_count).astype(jnp.float32)
    value_heads = value_frames.reshape(key_count, HEADS, HEAD_DIM, cell_count).astype(jnp.float32)
    scores = jnp.einsum('thdp,shdp->tshp', query_heads, key_heads) * HEAD_DIM ** (-0.5)
    query_pos = first_query + jnp.arange(query_count, dtype=jnp.int32)
    key_pos = first_key + jnp.arange(key_count, dtype=jnp.int32)
    offset = key_pos[None, :, None] - query_pos[:, None, None]
    inside = (key_pos >= 0) & (key_pos < total_frames)
    allowed = (offset >= -win_left[None, None, :]) & (offset <= win_right[None, None, :]) & inside[None, :, None]
    masked = jnp.where(allowed[..., None], scores, -1e+30)
    highest = lax.optimization_barrier(jnp.max(masked, axis=1, keepdims=True))
    raised = jnp.exp(masked - highest)
    weights = (raised / lax.optimization_barrier(jnp.sum(raised, axis=1, keepdims=True))).astype(jnp.bfloat16)
    blended = jnp.einsum('tshp,shdp->thdp', weights.astype(jnp.float32), value_heads)
    return blended.reshape(query_count, HEADS * HEAD_DIM, cell_count).astype(jnp.bfloat16)

def reference(frames_in, conv_spatial, conv_temporal, w_query, w_key, w_value, w_out, win_left, win_right):
    block_count = FRAMES // F_DEV
    cell_count = ROWS * WIDE

    def first_block(source):
        active = silu_round(source)
        lattice = active.reshape(F_DEV, C, ROWS, WIDE)
        padded = jnp.pad(lattice, ((0, 0), (0, 0), (1, 1), (1, 1)))
        tap_list = [padded[:, :, row_step:row_step + ROWS, col_step:col_step + WIDE] for row_step in range(3) for col_step in range(3)]
        stacked = jnp.concatenate(tap_list, axis=1).astype(jnp.float32)
        spatial = jnp.einsum('oj,fjrw->forw', conv_spatial.astype(jnp.float32), stacked).reshape(F_DEV, C, cell_count)
        settled = (source.astype(jnp.float32) + spatial).astype(jnp.bfloat16)
        return (settled, silu_round(settled))
    settled, moving = lax.map(first_block, frames_in.reshape(block_count, F_DEV, C, cell_count))
    settled = settled.reshape(FRAMES, C, cell_count)
    moving = jnp.pad(moving.reshape(FRAMES, C, cell_count), ((1, 1), (0, 0), (0, 0)))
    block_ids = jnp.arange(block_count, dtype=jnp.int32)

    def second_block(block_id):
        first_frame = (block_id * F_DEV).astype(jnp.int32)
        window = lax.dynamic_slice_in_dim(moving, first_frame, F_DEV + 2, 0)
        stacked = jnp.concatenate([window[0:F_DEV], window[1:F_DEV + 1], window[2:F_DEV + 2]], axis=1).astype(jnp.float32)
        temporal = jnp.einsum('oj,fjp->fop', conv_temporal.astype(jnp.float32), stacked)
        own_rows = lax.dynamic_slice_in_dim(settled, first_frame, F_DEV, 0)
        stream = (own_rows.astype(jnp.float32) + temporal).astype(jnp.bfloat16)
        normed = layer_norm(stream)
        return (stream, project(w_query, normed), project(w_key, normed), project(w_value, normed))
    stream, queries, key_frames, value_frames = lax.map(second_block, block_ids)
    stream = stream.reshape(FRAMES, C, cell_count)
    queries = queries.reshape(FRAMES, C, cell_count)
    key_frames = jnp.pad(key_frames.reshape(FRAMES, C, cell_count), ((WMAX, WMAX), (0, 0), (0, 0)))
    value_frames = jnp.pad(value_frames.reshape(FRAMES, C, cell_count), ((WMAX, WMAX), (0, 0), (0, 0)))

    def third_block(block_id):
        first_frame = (block_id * F_DEV).astype(jnp.int32)
        own_queries = lax.dynamic_slice_in_dim(queries, first_frame, F_DEV, 0)
        near_keys = lax.dynamic_slice_in_dim(key_frames, first_frame, F_DEV + 2 * WMAX, 0)
        near_values = lax.dynamic_slice_in_dim(value_frames, first_frame, F_DEV + 2 * WMAX, 0)
        blended = attend(own_queries, near_keys, near_values, first_frame, first_frame - WMAX, win_left, win_right, FRAMES)
        own_stream = lax.dynamic_slice_in_dim(stream, first_frame, F_DEV, 0)
        mixed_out = jnp.einsum('oi,fip->fop', w_out.astype(jnp.float32), blended.astype(jnp.float32))
        return (own_stream.astype(jnp.float32) + mixed_out).astype(jnp.bfloat16)
    return lax.map(third_block, block_ids).reshape(FRAMES, C, cell_count)
```

```python
import functools

import jax
import jax.numpy as jnp
from jax import lax
from jax.experimental import pallas as pl
from jax.experimental.pallas import tpu as pltpu
from jax.sharding import PartitionSpec as P

HEADS = 5
HEAD_DIM = 64
WIDE = 32
WMAX = 8
C = 320
F = 4
LANES = 128
MESH = pl.DeviceIdType.MESH
F32 = jnp.float32
BF16 = jnp.bfloat16
PAIRS = ((0, 3), (1, 2))
ORDER = (1, 2, 0, 3)


def silu(v):
    return 0.5 * v * (1.0 + jnp.tanh(0.5 * v))


def roll(v, shift):
    shift = shift % LANES
    return v if shift == 0 else pltpu.roll(v, shift, 1)


def kernel(
    frame_total,
    wl_ref,
    wr_ref,
    x_hbm,
    cs_hbm,
    ct_hbm,
    wq_hbm,
    wk_hbm,
    wv_hbm,
    wo_hbm,
    out_ref,
    x_ref,
    cs_ref,
    ct_ref,
    wqkv_ref,
    wo_ref,
    hsend,
    hrecv,
    active_ref,
    xcol,
    part_ref,
    settled_ref,
    moving_ref,
    stream_ref,
    near_ref,
    q_ref,
    k_ref,
    v_ref,
    acc_ref,
    m_ref,
    l_ref,
    load_sem,
    hs_sem,
    hr_sem,
    ts_sem,
    tr_sem,
    gs_sem,
    gr_sem,
):
    nt = lax.axis_size("tm")
    nh = lax.axis_size("height")
    it = lax.axis_index("tm")
    ih = lax.axis_index("height")
    t_next, t_prev = lax.rem(it + 1, nt), lax.rem(it + nt - 1, nt)
    h_next, h_prev = lax.rem(ih + 1, nh), lax.rem(ih + nh - 1, nh)

    loads = []
    for n, (src, dst) in enumerate(
        (
            (x_hbm, x_ref),
            (cs_hbm, cs_ref),
            (ct_hbm, ct_ref),
            (wq_hbm, wqkv_ref.at[pl.ds(0, C)]),
            (wk_hbm, wqkv_ref.at[pl.ds(C, C)]),
            (wv_hbm, wqkv_ref.at[pl.ds(2 * C, C)]),
            (wo_hbm, wo_ref),
        )
    ):
        copy = pltpu.make_async_copy(src, dst, load_sem.at[n])
        copy.start()
        loads.append(copy)

    barrier = pltpu.get_barrier_semaphore()
    for dev in ((t_next, ih), (t_prev, ih), (it, h_next), (it, h_prev)):
        pl.semaphore_signal(barrier, inc=1, device_id=dev, device_id_type=MESH)

    def remote(src, dst, ssem, rsem, dev):
        return pltpu.make_async_remote_copy(
            src_ref=src, dst_ref=dst, send_sem=ssem, recv_sem=rsem, device_id=dev, device_id_type=MESH
        )

    lane = lax.broadcasted_iota(jnp.int32, (C, LANES), 1)
    col = jnp.bitwise_and(lane, WIDE - 1)
    group = lax.shift_right_logical(lane, 5)

    loads[0].wait()
    top = jnp.zeros((C, LANES), F32)
    bottom = jnp.zeros((C, LANES), F32)
    for f in range(F):
        act = silu(x_ref[f].astype(F32))
        active_ref[f] = act
        top = jnp.where(group == f, roll(act, WIDE * f), top)
        bottom = jnp.where(group == f, roll(act, WIDE * f - 96), bottom)
    hsend[0] = bottom.astype(BF16)
    hsend[1] = top.astype(BF16)
    pl.semaphore_wait(barrier, 4)
    row_down = remote(hsend.at[0], hrecv.at[0], hs_sem.at[0], hr_sem.at[0], (it, h_next))
    row_up = remote(hsend.at[1], hrecv.at[1], hs_sem.at[1], hr_sem.at[1], (it, h_prev))
    row_down.start()
    row_up.start()

    def fill(n, k, a, rows):
        lanes = pl.ds(LANES * k, LANES)
        base = 3 * a * C
        xcol[n, pl.ds(base, C), lanes] = jnp.where(col == 0, 0.0, roll(rows, 1)).astype(BF16)
        xcol[n, pl.ds(base + C, C), lanes] = rows.astype(BF16)
        xcol[n, pl.ds(base + 2 * C, C), lanes] = jnp.where(col == WIDE - 1, 0.0, roll(rows, -1)).astype(BF16)

    for n in range(2):
        for k, f in enumerate(PAIRS[n]):
            fill(n, k, 1, active_ref[f])
    loads[1].wait()
    for n in range(2):
        part_ref[n] = jnp.dot(
            cs_ref[:, 1024:1920], xcol[n, pl.ds(1024, 896), :], preferred_element_type=F32
        )

    row_down.wait_recv()
    row_up.wait_recv()
    above = jnp.where(ih > 0, hrecv[0].astype(F32), 0.0)
    below = jnp.where(ih < nh - 1, hrecv[1].astype(F32), 0.0)

    def settle(n):
        for k, f in enumerate(PAIRS[n]):
            act = active_ref[f]
            fill(n, k, 0, jnp.where(group == 0, roll(above, -WIDE * f), roll(act, WIDE)))
            fill(n, k, 2, jnp.where(group == 3, roll(below, 96 - WIDE * f), roll(act, -WIDE)))
        total = part_ref[n]
        total += jnp.dot(cs_ref[:, 0:1024], xcol[n, pl.ds(0, 1024), :], preferred_element_type=F32)
        total += jnp.dot(cs_ref[:, 1920:2880], xcol[n, pl.ds(1920, 960), :], preferred_element_type=F32)
        for k, f in enumerate(PAIRS[n]):
            settled = (x_ref[f].astype(F32) + total[:, LANES * k : LANES * (k + 1)]).astype(BF16)
            settled_ref[f] = settled
            moving_ref[f + 1] = silu(settled.astype(F32)).astype(BF16)

    settle(0)
    to_next = remote(moving_ref.at[F], moving_ref.at[0], ts_sem.at[0], tr_sem.at[0], (t_next, ih))
    to_prev = remote(moving_ref.at[1], moving_ref.at[F + 1], ts_sem.at[1], tr_sem.at[1], (t_prev, ih))
    to_next.start()
    to_prev.start()
    settle(1)

    def gather(step, direction):
        f = ORDER[step % F]
        if direction == 0:
            src = 8 + f if step < F else 4 + f
            dst, dev = src - 4, (t_next, ih)
        else:
            src = 8 + f if step < F else 12 + f
            dst, dev = src + 4, (t_prev, ih)
        return remote(
            near_ref.at[src], near_ref.at[dst], gs_sem.at[direction, step], gr_sem.at[direction, step], dev
        )

    def temporal(n):
        stacked = jnp.concatenate(
            [moving_ref[pl.ds(f, 3)].reshape(3 * C, LANES) for f in PAIRS[n]], axis=1
        )
        total = jnp.dot(ct_ref[...], stacked, preferred_element_type=F32)
        for k, f in enumerate(PAIRS[n]):
            stream = (settled_ref[f].astype(F32) + total[:, LANES * k : LANES * (k + 1)]).astype(BF16)
            stream_ref[f] = stream
            wide = stream.astype(F32)
            centred = wide - jnp.sum(wide, axis=0, keepdims=True) * (1.0 / C)
            spread = jnp.sum(centred * centred, axis=0, keepdims=True) * (1.0 / C)
            near_ref[8 + f] = (centred * lax.rsqrt(spread + 1e-05)).astype(BF16)

    loads[2].wait()
    temporal(1)
    copies = {}
    for step in (0, 1):
        for direction in (0, 1):
            copies[step, direction] = gather(step, direction)
            copies[step, direction].start()
    to_next.wait_recv()
    to_prev.wait_recv()

    @pl.when(it == 0)
    def _():
        moving_ref[0] = jnp.zeros((C, LANES), BF16)

    @pl.when(it == nt - 1)
    def _():
        moving_ref[F + 1] = jnp.zeros((C, LANES), BF16)

    temporal(0)
    for step in (2, 3):
        for direction in (0, 1):
            copies[step, direction] = gather(step, direction)
            copies[step, direction].start()

    for n in (3, 4, 5):
        loads[n].wait()

    def joined(first):
        return jnp.concatenate([near_ref[first + f] for f in range(F)], axis=1)

    own = joined(8)
    made = jnp.dot(wqkv_ref[pl.ds(0, C)], own, preferred_element_type=F32)
    for f in range(F):
        q_ref[f] = (made[:, LANES * f : LANES * (f + 1)]).astype(BF16)

    def keys(first):
        near = joined(first)
        made = jnp.dot(wqkv_ref[pl.ds(C, 2 * C)], near, preferred_element_type=F32)
        for f in range(F):
            part = made[:, LANES * f : LANES * (f + 1)].astype(BF16)
            k_ref[f] = part[:C]
            v_ref[f] = part[C:]

    head_row = lax.broadcasted_iota(jnp.int32, (8, LANES), 0)
    reach_left = jnp.zeros((8, LANES), jnp.int32)
    reach_right = jnp.zeros((8, LANES), jnp.int32)
    for h in range(HEADS):
        reach_left = jnp.where(head_row == h, wl_ref[h], reach_left)
        reach_right = jnp.where(head_row == h, wr_ref[h], reach_right)
    summing = jnp.where(
        lax.shift_right_logical(lax.broadcasted_iota(jnp.int32, (16, C), 1), 6)
        == lax.broadcasted_iota(jnp.int32, (16, C), 0),
        1.0,
        0.0,
    ).astype(BF16)

    def attend(first, fresh):
        keys(first)

        def step(t, carry):
            query = q_ref[t]
            products = jnp.concatenate([query * k_ref[s] for s in range(F)], axis=1)
            scores = jnp.dot(summing, products, preferred_element_type=F32)[:8] * HEAD_DIM ** (-0.5)
            masked = []
            for s in range(F):
                offset = first - 8 + s - t
                position = F * it + (first - 8 + s)
                inside = (position >= 0) & (position < frame_total)
                far = jnp.where(inside, offset, 2 * WMAX + F)
                allowed = (far >= -reach_left) & (far <= reach_right)
                masked.append(jnp.where(allowed, scores[:, LANES * s : LANES * (s + 1)], -1e30))
            highest = jnp.maximum(jnp.maximum(masked[0], masked[1]), jnp.maximum(masked[2], masked[3]))
            if not fresh:
                before = m_ref[t]
                highest = jnp.maximum(highest, before)
                fade = jnp.exp(before - highest)
            raised = [jnp.exp(one - highest) for one in masked]
            total = (raised[0] + raised[1]) + (raised[2] + raised[3])
            if not fresh:
                total = total + l_ref[t] * fade
            m_ref[t] = highest
            l_ref[t] = total
            for h in range(HEADS):
                rows = pl.ds(HEAD_DIM * h, HEAD_DIM)
                acc = raised[0][h : h + 1] * v_ref[0, rows].astype(F32)
                for s in range(1, F):
                    acc += raised[s][h : h + 1] * v_ref[s, rows].astype(F32)
                if not fresh:
                    acc += acc_ref[t, rows] * fade[h : h + 1]
                acc_ref[t, rows] = acc
            return carry

        lax.fori_loop(0, F, step, 0)

    attend(8, True)

    for step in range(F):
        for direction in (0, 1):
            copies[step, direction].wait_recv()
            copies[step + F, direction] = gather(step + F, direction)
            copies[step + F, direction].start()
    attend(4, False)
    attend(12, False)
    for step in range(F, 2 * F):
        copies[step, 0].wait_recv()
    attend(0, False)
    for step in range(F, 2 * F):
        copies[step, 1].wait_recv()
    attend(16, False)

    loads[6].wait()
    blended = []
    for t in range(F):
        scale = 1.0 / l_ref[t]
        blended.append(
            jnp.concatenate(
                [
                    (acc_ref[t, pl.ds(HEAD_DIM * h, HEAD_DIM)] * scale[h : h + 1]).astype(BF16)
                    for h in range(HEADS)
                ],
                axis=0,
            )
        )
    mixed = jnp.dot(wo_ref[...], jnp.concatenate(blended, axis=1), preferred_element_type=F32)
    for t in range(F):
        out_ref[t] = (stream_ref[t].astype(F32) + mixed[:, LANES * t : LANES * (t + 1)]).astype(BF16)

    row_down.wait_send()
    row_up.wait_send()
    to_next.wait_send()
    to_prev.wait_send()
    for step in range(2 * F):
        for direction in (0, 1):
            copies[step, direction].wait_send()


def per_device(
    frames_in, conv_spatial, conv_temporal, w_query, w_key, w_value, w_out, win_left, win_right
):
    smem = pl.BlockSpec(memory_space=pltpu.SMEM)
    hbm = pl.BlockSpec(memory_space=pl.ANY)
    frame_total = F * lax.axis_size("tm")
    frame = (C, LANES)
    return pl.pallas_call(
        functools.partial(kernel, frame_total),
        out_shape=jax.ShapeDtypeStruct(frames_in.shape, BF16),
        in_specs=[smem, smem] + [hbm] * 7,
        out_specs=pl.BlockSpec(memory_space=pltpu.VMEM),
        scratch_shapes=[
            pltpu.VMEM((F,) + frame, BF16),
            pltpu.VMEM((C, 9 * C), BF16),
            pltpu.VMEM((C, 3 * C), BF16),
            pltpu.VMEM((3 * C, C), BF16),
            pltpu.VMEM((C, C), BF16),
            pltpu.VMEM((2,) + frame, BF16),
            pltpu.VMEM((2,) + frame, BF16),
            pltpu.VMEM((F,) + frame, F32),
            pltpu.VMEM((2, 9 * C, 2 * LANES), BF16),
            pltpu.VMEM((2, C, 2 * LANES), F32),
            pltpu.VMEM((F,) + frame, BF16),
            pltpu.VMEM((F + 2,) + frame, BF16),
            pltpu.VMEM((F,) + frame, BF16),
            pltpu.VMEM((F + 2 * WMAX,) + frame, BF16),
            pltpu.VMEM((F,) + frame, BF16),
            pltpu.VMEM((F,) + frame, BF16),
            pltpu.VMEM((F,) + frame, BF16),
            pltpu.VMEM((F,) + frame, F32),
            pltpu.VMEM((F, 8, LANES), F32),
            pltpu.VMEM((F, 8, LANES), F32),
            pltpu.SemaphoreType.DMA((7,)),
            pltpu.SemaphoreType.DMA((2,)),
            pltpu.SemaphoreType.DMA((2,)),
            pltpu.SemaphoreType.DMA((2,)),
            pltpu.SemaphoreType.DMA((2,)),
            pltpu.SemaphoreType.DMA((2, 2 * F)),
            pltpu.SemaphoreType.DMA((2, 2 * F)),
        ],
        compiler_params=pltpu.CompilerParams(
            collective_id=0, has_side_effects=True, vmem_limit_bytes=48 * 1024 * 1024
        ),
    )(win_left, win_right, frames_in, conv_spatial, conv_temporal, w_query, w_key, w_value, w_out)


def solution(mesh):
    return jax.shard_map(
        per_device,
        mesh=mesh,
        in_specs=(P("tm", None, "height"), P(), P(), P(), P(), P(), P(), P(), P()),
        out_specs=P("tm", None, "height"),
        check_vma=False,
    )
```

```python
import functools

import jax
import jax.numpy as jnp
from jax import lax
from jax.experimental import pallas as pl
from jax.experimental.pallas import tpu as pltpu
from jax.sharding import PartitionSpec as P

HEADS = 5
HEAD_DIM = 64
WIDE = 32
C = 320
F = 4
LANES = 128
MESH = pl.DeviceIdType.MESH
F32 = jnp.float32
BF16 = jnp.bfloat16
PAIRS = ((0, 3), (1, 2))


def silu(v):
    return 0.5 * v * (1.0 + jnp.tanh(0.5 * v))


def roll(v, shift):
    shift = shift % LANES
    return v if shift == 0 else pltpu.roll(v, shift, 1)


def kernel(
    wl_hbm,
    wr_hbm,
    x_hbm,
    cs_hbm,
    ct_hbm,
    wq_hbm,
    wk_hbm,
    wv_hbm,
    wo_hbm,
    out_ref,
    x_ref,
    cs_ref,
    ct_ref,
    wqkv_ref,
    wo_ref,
    hsend,
    hrecv,
    active_ref,
    xcol,
    part_ref,
    settled_ref,
    moving_ref,
    stream_ref,
    normed_ref,
    packed_ref,
    blended_ref,
    back_ref,
    near_ref,
    q_ref,
    k_ref,
    v_ref,
    acc_ref,
    m_ref,
    l_ref,
    wl_ref,
    wr_ref,
    load_sem,
    hs_sem,
    hr_sem,
    ts_sem,
    tr_sem,
    gs_sem,
    gr_sem,
    zs_sem,
    zr_sem,
    bs_sem,
    br_sem,
):
    nt = lax.axis_size("tm")
    nh = lax.axis_size("height")
    it = lax.axis_index("tm")
    ih = lax.axis_index("height")
    t_next, t_prev = lax.rem(it + 1, nt), lax.rem(it + nt - 1, nt)
    h_next, h_prev = lax.rem(ih + 1, nh), lax.rem(ih + nh - 1, nh)

    team, mine, teams = it // F, lax.rem(it, F), nt // F

    loads = []
    for n, (src, dst) in enumerate(
        (
            (x_hbm, x_ref),
            (cs_hbm, cs_ref),
            (ct_hbm, ct_ref),
            (wq_hbm, wqkv_ref.at[pl.ds(0, C)]),
            (wk_hbm, wqkv_ref.at[pl.ds(C, C)]),
            (wv_hbm, wqkv_ref.at[pl.ds(2 * C, C)]),
            (wo_hbm, wo_ref),
            (wl_hbm, wl_ref),
            (wr_hbm, wr_ref),
        )
    ):
        copy = pltpu.make_async_copy(src, dst, load_sem.at[n])
        copy.start()
        loads.append(copy)

    barrier = pltpu.get_barrier_semaphore()
    friends = [(t_next, ih), (t_prev, ih), (it, h_next), (it, h_prev)]
    friends += [(F * team + lax.rem(mine + step, F), ih) for step in (1, 2, 3)]
    friends += [(lax.rem(it + F, nt), ih), (lax.rem(it + nt - F, nt), ih)]
    for dev in friends:
        pl.semaphore_signal(barrier, inc=1, device_id=dev, device_id_type=MESH)

    def remote(src, dst, ssem, rsem, dev):
        return pltpu.make_async_remote_copy(
            src_ref=src, dst_ref=dst, send_sem=ssem, recv_sem=rsem, device_id=dev, device_id_type=MESH
        )

    lane = lax.broadcasted_iota(jnp.int32, (C, LANES), 1)
    col = jnp.bitwise_and(lane, WIDE - 1)
    group = lax.shift_right_logical(lane, 5)

    loads[0].wait()
    top = jnp.zeros((C, LANES), F32)
    bottom = jnp.zeros((C, LANES), F32)
    for f in range(F):
        act = silu(x_ref[f].astype(F32))
        active_ref[f] = act
        top = jnp.where(group == f, roll(act, WIDE * f), top)
        bottom = jnp.where(group == f, roll(act, WIDE * f - 96), bottom)
    hsend[0] = bottom.astype(BF16)
    hsend[1] = top.astype(BF16)
    pl.semaphore_wait(barrier, len(friends))
    row_down = remote(hsend.at[0], hrecv.at[0], hs_sem.at[0], hr_sem.at[0], (it, h_next))
    row_up = remote(hsend.at[1], hrecv.at[1], hs_sem.at[1], hr_sem.at[1], (it, h_prev))
    row_down.start()
    row_up.start()

    def fill(n, k, a, rows):
        lanes = pl.ds(LANES * k, LANES)
        base = 3 * a * C
        xcol[n, pl.ds(base, C), lanes] = jnp.where(col == 0, 0.0, roll(rows, 1)).astype(BF16)
        xcol[n, pl.ds(base + C, C), lanes] = rows.astype(BF16)
        xcol[n, pl.ds(base + 2 * C, C), lanes] = jnp.where(col == WIDE - 1, 0.0, roll(rows, -1)).astype(BF16)

    for n in range(2):
        for k, f in enumerate(PAIRS[n]):
            fill(n, k, 1, active_ref[f])
    loads[1].wait()
    for n in range(2):
        part_ref[n] = jnp.dot(
            cs_ref[:, 1024:1920], xcol[n, pl.ds(1024, 896), :], preferred_element_type=F32
        )

    row_down.wait_recv()
    row_up.wait_recv()
    above = jnp.where(ih > 0, hrecv[0].astype(F32), 0.0)
    below = jnp.where(ih < nh - 1, hrecv[1].astype(F32), 0.0)

    def settle(n):
        for k, f in enumerate(PAIRS[n]):
            act = active_ref[f]
            fill(n, k, 0, jnp.where(group == 0, roll(above, -WIDE * f), roll(act, WIDE)))
            fill(n, k, 2, jnp.where(group == 3, roll(below, 96 - WIDE * f), roll(act, -WIDE)))
        total = part_ref[n]
        total += jnp.dot(cs_ref[:, 0:1024], xcol[n, pl.ds(0, 1024), :], preferred_element_type=F32)
        total += jnp.dot(cs_ref[:, 1920:2880], xcol[n, pl.ds(1920, 960), :], preferred_element_type=F32)
        for k, f in enumerate(PAIRS[n]):
            settled = (x_ref[f].astype(F32) + total[:, LANES * k : LANES * (k + 1)]).astype(BF16)
            settled_ref[f] = settled
            moving_ref[f + 1] = silu(settled.astype(F32)).astype(BF16)

    settle(0)
    to_next = remote(moving_ref.at[F], moving_ref.at[0], ts_sem.at[0], tr_sem.at[0], (t_next, ih))
    to_prev = remote(moving_ref.at[1], moving_ref.at[F + 1], ts_sem.at[1], tr_sem.at[1], (t_prev, ih))

    @pl.when(it < nt - 1)
    def _():
        to_next.start()

    @pl.when(it > 0)
    def _():
        to_prev.start()

    settle(1)

    def temporal(n):
        stacked = jnp.concatenate(
            [moving_ref[pl.ds(f, 3)].reshape(3 * C, LANES) for f in PAIRS[n]], axis=1
        )
        total = jnp.dot(ct_ref[...], stacked, preferred_element_type=F32)
        for k, f in enumerate(PAIRS[n]):
            stream = (settled_ref[f].astype(F32) + total[:, LANES * k : LANES * (k + 1)]).astype(BF16)
            stream_ref[f] = stream
            wide = stream.astype(F32)
            centred = wide - jnp.sum(wide, axis=0, keepdims=True) * (1.0 / C)
            spread = jnp.sum(centred * centred, axis=0, keepdims=True) * (1.0 / C)
            normed_ref[f] = centred * lax.rsqrt(spread + 1e-05)

    loads[2].wait()
    temporal(1)

    @pl.when(it > 0)
    def _():
        to_next.wait_recv()

    @pl.when(it < nt - 1)
    def _():
        to_prev.wait_recv()

    @pl.when(it == 0)
    def _():
        moving_ref[0] = jnp.zeros((C, LANES), BF16)

    @pl.when(it == nt - 1)
    def _():
        moving_ref[F + 1] = jnp.zeros((C, LANES), BF16)

    temporal(0)

    for j in range(F):
        row = jnp.zeros((C, LANES), F32)
        for f in range(F):
            row = jnp.where(group == f, roll(normed_ref[f], WIDE * (f - j)), row)
        packed_ref[j] = row.astype(BF16)

    def swap(step):
        other = lax.rem(mine + step, F)
        return remote(
            packed_ref.at[other],
            near_ref.at[2 + mine],
            gs_sem.at[step],
            gr_sem.at[mine],
            (F * team + other, ih),
        )

    def swapped(member):
        return remote(
            packed_ref.at[0], near_ref.at[2 + member], gs_sem.at[0], gr_sem.at[member], (it, h_next)
        )

    swaps = [swap(step) for step in (2, 1, 3)]
    for copy in swaps:
        copy.start()
    near_ref[2 + mine] = packed_ref[mine]

    def halo(member):
        late = member >= 2
        place = jnp.where(late, member - 2, member + 6)
        dev = (jnp.where(late, lax.rem(it + F, nt), lax.rem(it + nt - F, nt)), ih)
        return late, remote(
            near_ref.at[2 + member], near_ref.at[place], zs_sem.at[member], zr_sem.at[place], dev
        )

    def wanted(late):
        return jnp.where(late, jnp.where(team < teams - 1, 1, 0), jnp.where(team > 0, 1, 0)) == 1

    halos = []

    def send_halo(member):
        late, copy = halo(member)
        halos.append((late, copy))

        @pl.when(wanted(late))
        def _():
            copy.start()

    send_halo(mine)
    for n in (3, 4, 5, 7, 8):
        loads[n].wait()
    for step in (1, 3, 2):
        member = lax.rem(mine + step, F)
        swapped(member).wait_recv()
        send_halo(member)

    own = jnp.concatenate([near_ref[2 + i] for i in range(F)], axis=1)
    made = jnp.dot(wqkv_ref[...], own, preferred_element_type=F32)
    for i in range(F):
        part = made[:, LANES * i : LANES * (i + 1)]
        for r in range(F):
            q_ref[r, i] = roll(part[:C], WIDE * r).astype(BF16)
            v_ref[r, 2 + i] = roll(part[2 * C :], -WIDE * r).astype(BF16)
        k_ref[2 + i] = part[C : 2 * C].astype(BF16)

    def keys(first):
        near = jnp.concatenate([near_ref[first], near_ref[first + 1]], axis=1)
        made = jnp.dot(wqkv_ref[pl.ds(C, 2 * C)], near, preferred_element_type=F32)
        for i in range(2):
            part = made[:, LANES * i : LANES * (i + 1)]
            k_ref[first + i] = part[:C].astype(BF16)
            for r in range(F):
                v_ref[r, first + i] = roll(part[C:], -WIDE * r).astype(BF16)

    head_row = lax.broadcasted_iota(jnp.int32, (8, LANES), 0)
    lane_frame = lax.shift_right_logical(lax.broadcasted_iota(jnp.int32, (8, LANES), 1), 5)
    reach_left = jnp.zeros((8, LANES), jnp.int32)
    reach_right = jnp.zeros((8, LANES), jnp.int32)
    for h in range(HEADS):
        reach_left = jnp.where(head_row == h, wl_ref[h], reach_left)
        reach_right = jnp.where(head_row == h, wr_ref[h], reach_right)
    summing = jnp.where(
        lax.shift_right_logical(lax.broadcasted_iota(jnp.int32, (16, C), 1), 6)
        == lax.broadcasted_iota(jnp.int32, (16, C), 0),
        1.0,
        0.0,
    ).astype(BF16)

    def attend(i, blocks, fresh):
        masked = []
        for m in blocks:
            products = jnp.concatenate([q_ref[r, i] * k_ref[m] for r in range(F)], axis=1)
            scores = jnp.dot(summing, products, preferred_element_type=F32)[:8] * HEAD_DIM ** (-0.5)
            for r in range(F):
                turned = roll(scores[:, LANES * r : LANES * (r + 1)], -WIDE * r)
                offset = F * (m - 2 - i) + jnp.bitwise_and(lane_frame + r, F - 1) - lane_frame
                allowed = (offset >= -reach_left) & (offset <= reach_right)
                masked.append(jnp.where(allowed, turned, -1e30))
        highest = functools.reduce(jnp.maximum, masked)
        if not fresh:
            before = m_ref[i]
            highest = jnp.maximum(highest, before)
            fade = jnp.exp(before - highest)
        raised = [jnp.exp(one - highest) for one in masked]
        total = functools.reduce(jnp.add, raised)
        if not fresh:
            total = total + l_ref[i] * fade
        m_ref[i] = highest
        l_ref[i] = total
        for h in range(HEADS):
            rows = pl.ds(HEAD_DIM * h, HEAD_DIM)
            acc = None if fresh else acc_ref[i, rows] * fade[h : h + 1]
            for n, m in enumerate(blocks):
                for r in range(F):
                    term = raised[F * n + r][h : h + 1] * v_ref[r, m, rows].astype(F32)
                    acc = term if acc is None else acc + term
            acc_ref[i, rows] = acc

    def loop(low, high, blocks, fresh):
        def step(i, carry):
            attend(i, blocks, fresh)
            return carry

        lax.fori_loop(low, high, step, 0)

    def finish(i):
        scale = 1.0 / l_ref[i]
        blended_ref[i] = jnp.concatenate(
            [
                (acc_ref[i, pl.ds(HEAD_DIM * h, HEAD_DIM)] * scale[h : h + 1]).astype(BF16)
                for h in range(HEADS)
            ],
            axis=0,
        )
        copy = remote(
            blended_ref.at[i], back_ref.at[mine], bs_sem.at[i], br_sem.at[mine], (F * team + i, ih)
        )

        @pl.when(mine != i)
        def _():
            copy.start()

        @pl.when(mine == i)
        def _():
            back_ref[mine] = blended_ref[i]

        return copy

    loop(0, F, (2, 3, 4, 5), True)

    def received(place):
        remote(near_ref.at[2], near_ref.at[place], zs_sem.at[0], zr_sem.at[place], (it, h_next)).wait_recv()

    @pl.when(team > 0)
    def _():
        received(0)
        received(1)
        keys(0)
        loop(0, 2, (0, 1), False)

    backs = [finish(0), finish(1)]

    @pl.when(team < teams - 1)
    def _():
        received(6)
        received(7)
        keys(6)
        loop(2, 4, (6, 7), False)

    backs += [finish(2), finish(3)]

    loads[6].wait()
    for step in (1, 3, 2):
        member = lax.rem(mine + step, F)
        remote(
            blended_ref.at[0], back_ref.at[member], bs_sem.at[0], br_sem.at[member], (it, h_next)
        ).wait_recv()
    mixed = jnp.dot(
        wo_ref[...],
        jnp.concatenate([back_ref[j] for j in range(F)], axis=1),
        preferred_element_type=F32,
    )
    for f in range(F):
        whole = jnp.zeros((C, LANES), F32)
        for j in range(F):
            whole = jnp.where(group == j, roll(mixed[:, LANES * j : LANES * (j + 1)], WIDE * (j - f)), whole)
        out_ref[f] = (stream_ref[f].astype(F32) + whole).astype(BF16)

    row_down.wait_send()
    row_up.wait_send()

    @pl.when(it < nt - 1)
    def _():
        to_next.wait_send()

    @pl.when(it > 0)
    def _():
        to_prev.wait_send()

    for copy in swaps:
        copy.wait_send()
    for late, copy in halos:

        @pl.when(wanted(late))
        def _():
            copy.wait_send()

    for i in range(F):

        @pl.when(mine != i)
        def _():
            backs[i].wait_send()


def per_device(
    frames_in, conv_spatial, conv_temporal, w_query, w_key, w_value, w_out, win_left, win_right
):
    hbm = pl.BlockSpec(memory_space=pltpu.HBM)
    frame = (C, LANES)
    return pl.pallas_call(
        kernel,
        out_shape=jax.ShapeDtypeStruct(frames_in.shape, BF16),
        in_specs=[hbm] * 9,
        out_specs=pl.BlockSpec(memory_space=pltpu.VMEM),
        scratch_shapes=[
            pltpu.VMEM((F,) + frame, BF16),
            pltpu.VMEM((C, 9 * C), BF16),
            pltpu.VMEM((C, 3 * C), BF16),
            pltpu.VMEM((3 * C, C), BF16),
            pltpu.VMEM((C, C), BF16),
            pltpu.VMEM((2,) + frame, BF16),
            pltpu.VMEM((2,) + frame, BF16),
            pltpu.VMEM((F,) + frame, F32),
            pltpu.VMEM((2, 9 * C, 2 * LANES), BF16),
            pltpu.VMEM((2, C, 2 * LANES), F32),
            pltpu.VMEM((F,) + frame, BF16),
            pltpu.VMEM((F + 2,) + frame, BF16),
            pltpu.VMEM((F,) + frame, BF16),
            pltpu.VMEM((F,) + frame, F32),
            pltpu.VMEM((F,) + frame, BF16),
            pltpu.VMEM((F,) + frame, BF16),
            pltpu.VMEM((F,) + frame, BF16),
            pltpu.VMEM((2 * F,) + frame, BF16),
            pltpu.VMEM((F, F) + frame, BF16),
            pltpu.VMEM((2 * F,) + frame, BF16),
            pltpu.VMEM((F, 2 * F) + frame, BF16),
            pltpu.VMEM((F,) + frame, F32),
            pltpu.VMEM((F, 8, LANES), F32),
            pltpu.VMEM((F, 8, LANES), F32),
            pltpu.SMEM((HEADS,), jnp.int32),
            pltpu.SMEM((HEADS,), jnp.int32),
            pltpu.SemaphoreType.DMA((9,)),
            pltpu.SemaphoreType.DMA((2,)),
            pltpu.SemaphoreType.DMA((2,)),
            pltpu.SemaphoreType.DMA((2,)),
            pltpu.SemaphoreType.DMA((2,)),
            pltpu.SemaphoreType.DMA((F,)),
            pltpu.SemaphoreType.DMA((F,)),
            pltpu.SemaphoreType.DMA((F,)),
            pltpu.SemaphoreType.DMA((2 * F,)),
            pltpu.SemaphoreType.DMA((F,)),
            pltpu.SemaphoreType.DMA((F,)),
        ],
        compiler_params=pltpu.CompilerParams(
            collective_id=0, has_side_effects=True, vmem_limit_bytes=62 * 1024 * 1024
        ),
    )(win_left, win_right, frames_in, conv_spatial, conv_temporal, w_query, w_key, w_value, w_out)


def solution(mesh):
    return jax.shard_map(
        per_device,
        mesh=mesh,
        in_specs=(P("tm", None, "height"), P(), P(), P(), P(), P(), P(), P(), P()),
        out_specs=P("tm", None, "height"),
        check_vma=False,
    )
```

```python
import functools

import jax
import jax.numpy as jnp
from jax import lax
from jax.experimental import pallas as pl
from jax.experimental.pallas import tpu as pltpu
from jax.sharding import PartitionSpec as P

HEADS = 5
HEAD_DIM = 64
WIDE = 32
C = 320
F = 4
LANES = 128
QUARTER = C // F
MESH = pl.DeviceIdType.MESH
F32 = jnp.float32
BF16 = jnp.bfloat16


def silu(v):
    return 0.5 * v * (1.0 + jnp.tanh(0.5 * v))


def roll(v, shift):
    shift = shift % LANES
    return v if shift == 0 else pltpu.roll(v, shift, 1)


def kernel(
    wl_hbm,
    wr_hbm,
    x_hbm,
    cs_hbm,
    ct_hbm,
    wq_hbm,
    wk_hbm,
    wv_hbm,
    wo_hbm,
    out_ref,
    x_ref,
    cs_ref,
    ct_ref,
    wqkv_ref,
    wo_ref,
    wl_ref,
    wr_ref,
    rows_ref,
    taps_ref,
    above_ref,
    settled_ref,
    edge_ref,
    near_ref,
    far_ref,
    steps_ref,
    stream_ref,
    done_ref,
    back_ref,
    q_ref,
    k_ref,
    v_ref,
    acc_ref,
    m_ref,
    l_ref,
    load_sem,
    hs_sem,
    hr_sem,
    gs_sem,
    gr_sem,
    es_sem,
    er_sem,
    zs_sem,
    zr_sem,
    bs_sem,
    br_sem,
):
    nt = lax.axis_size("tm")
    nh = lax.axis_size("height")
    it = lax.axis_index("tm")
    ih = lax.axis_index("height")
    h_next, h_prev = lax.rem(ih + 1, nh), lax.rem(ih + nh - 1, nh)
    team, mine, teams = it // F, lax.rem(it, F), nt // F
    odd = lax.rem(mine, 2)
    later, earlier = lax.rem(team + 1, teams), lax.rem(team + teams - 1, teams)

    loads = []
    for n, (src, dst) in enumerate(
        (
            (x_hbm, x_ref),
            (cs_hbm, cs_ref),
            (ct_hbm, ct_ref),
            (wq_hbm, wqkv_ref.at[pl.ds(0, C)]),
            (wk_hbm, wqkv_ref.at[pl.ds(C, C)]),
            (wv_hbm, wqkv_ref.at[pl.ds(2 * C, C)]),
            (wo_hbm, wo_ref),
            (wl_hbm, wl_ref),
            (wr_hbm, wr_ref),
        )
    ):
        copy = pltpu.make_async_copy(src, dst, load_sem.at[n])
        copy.start()
        loads.append(copy)

    barrier = pltpu.get_barrier_semaphore()
    friends = [(it, h_next), (it, h_prev)]
    friends += [(F * team + lax.rem(mine + step, F), ih) for step in (1, 2, 3)]
    friends += [(F * later + mine, ih), (F * earlier + mine, ih)]
    friends += [(F * earlier + 1, ih), (F * earlier + 3, ih), (F * later, ih), (F * later + 2, ih)]
    for dev in friends:
        pl.semaphore_signal(barrier, inc=1, device_id=dev, device_id_type=MESH)

    def remote(src, dst, ssem, rsem, dev):
        return pltpu.make_async_remote_copy(
            src_ref=src, dst_ref=dst, send_sem=ssem, recv_sem=rsem, device_id=dev, device_id_type=MESH
        )

    lane = lax.broadcasted_iota(jnp.int32, (C, LANES), 1)
    col = jnp.bitwise_and(lane, WIDE - 1)
    group = lax.shift_right_logical(lane, 5)
    block_group = lax.shift_right_logical(lax.broadcasted_iota(jnp.int32, (QUARTER, LANES), 1), 5)

    def fill(place, act):
        taps_ref[place, pl.ds(0, C)] = jnp.where(col == 0, 0.0, roll(act, 1)).astype(BF16)
        taps_ref[place, pl.ds(C, C)] = act.astype(BF16)
        taps_ref[place, pl.ds(2 * C, C)] = jnp.where(col == WIDE - 1, 0.0, roll(act, -1)).astype(BF16)

    loads[0].wait()
    frames = [x_ref[f].astype(F32) for f in range(F)]
    for j in range(F):
        row = jnp.zeros((C, LANES), F32)
        for f in range(F):
            row = jnp.where(group == f, roll(frames[f], WIDE * (f - j)), row)
        rows_ref[j] = row
        fill(j + 1, silu(row))

    pl.semaphore_wait(barrier, len(friends))
    row_down = remote(
        taps_ref.at[F, pl.ds(C, C)], above_ref.at[0], hs_sem.at[0], hr_sem.at[0], (it, h_next)
    )
    row_up = remote(
        taps_ref.at[1, pl.ds(C, C)], above_ref.at[1], hs_sem.at[1], hr_sem.at[1], (it, h_prev)
    )
    row_down.start()
    row_up.start()

    def around(j):
        return taps_ref[pl.ds(j, 3)].reshape(9 * C, LANES)

    def product(weights, source):
        return jnp.dot(weights, source, preferred_element_type=F32)

    swaps, edges = {}, {}
    edge_team = jnp.where(odd == 1, later, earlier)
    edge_slot = jnp.where(odd == 1, 0, 2) + mine // 2
    edge_wanted = jnp.where(odd == 1, jnp.where(team < teams - 1, 1, 0), jnp.where(team > 0, 1, 0)) == 1

    def settle(j, spatial):
        settled = (rows_ref[j] + spatial).astype(BF16)
        settled_ref[j] = settled
        wide = settled.astype(F32)
        swaps[j] = remote(
            settled_ref.at[j], near_ref.at[2 + mine], gs_sem.at[j], gr_sem.at[mine], (F * team + j, ih)
        )

        @pl.when(mine != j)
        def _():
            swaps[j].start()

        @pl.when(mine == j)
        def _():
            near_ref[2 + j] = settled

        block = jnp.zeros((QUARTER, LANES), F32)
        for n in range(F):
            part = wide[QUARTER * n : QUARTER * (n + 1)]
            turned = jnp.where(odd == 1, roll(part, WIDE * (n + 1)), roll(part, WIDE * n))
            block = jnp.where(block_group == n, turned, block)
        edge_ref[j] = block.astype(BF16)
        edges[j] = remote(
            edge_ref.at[j], far_ref.at[edge_slot], es_sem.at[j], er_sem.at[edge_slot], (F * edge_team + j, ih)
        )

        @pl.when(edge_wanted)
        def _():
            edges[j].start()

    loads[1].wait()
    inner = product(cs_ref[...], jnp.concatenate([around(1), around(2)], axis=1))
    settle(1, inner[:, :LANES])
    settle(2, inner[:, LANES:])
    upper = product(cs_ref[:, 1024:2880], around(0)[1024:2880])
    lower = product(cs_ref[:, 0:1920], around(3)[0:1920])

    row_down.wait_recv()
    row_up.wait_recv()
    fill(0, jnp.where(ih > 0, above_ref[0].astype(F32), 0.0))
    fill(F + 1, jnp.where(ih < nh - 1, above_ref[1].astype(F32), 0.0))
    settle(0, upper + product(cs_ref[:, 0:1024], around(0)[0:1024]))
    settle(3, lower + product(cs_ref[:, 1920:2880], around(3)[1920:2880]))

    def swapped(member):
        return remote(
            settled_ref.at[0], near_ref.at[2 + member], gs_sem.at[0], gr_sem.at[member], (it, h_next)
        )

    def wanted(late):
        return jnp.where(late, jnp.where(team < teams - 1, 1, 0), jnp.where(team > 0, 1, 0)) == 1

    halos = []

    def send_halo(member):
        late = member >= 2
        place = jnp.where(late, member - 2, member + 6)
        copy = remote(
            near_ref.at[2 + member],
            near_ref.at[place],
            zs_sem.at[member],
            zr_sem.at[place],
            (F * jnp.where(late, later, earlier) + mine, ih),
        )
        halos.append((late, copy))

        @pl.when(wanted(late))
        def _():
            copy.start()

    send_halo(mine)
    for n in (2, 3, 4, 5, 6, 7, 8):
        loads[n].wait()
    for step in (1, 3, 2):
        member = lax.rem(mine + step, F)
        swapped(member).wait_recv()
        send_halo(member)

    def edge_arrived(slot):
        remote(edge_ref.at[0], far_ref.at[slot], es_sem.at[0], er_sem.at[slot], (it, h_next)).wait_recv()

    def halo_arrived(place):
        remote(near_ref.at[2], near_ref.at[place], zs_sem.at[0], zr_sem.at[place], (it, h_next)).wait_recv()

    @pl.when(team > 0)
    def _():
        edge_arrived(1)

    @pl.when(team < teams - 1)
    def _():
        edge_arrived(2)

    def edge_frame(slot, there, place):
        block = silu(jnp.where(there, far_ref[slot].astype(F32), 0.0))
        return jnp.concatenate([roll(block, WIDE * (place - n)) for n in range(F)], axis=0)

    def temporal(first, count, before, after):
        ahead, behind = [], []
        for m in range(count):
            moving = silu(near_ref[first + m].astype(F32))
            steps_ref[m, pl.ds(C, C)] = moving.astype(BF16)
            ahead.append(roll(moving, WIDE))
            behind.append(roll(moving, -WIDE))
        for m in range(count):
            left = before if m == 0 else ahead[m - 1]
            right = after if m == count - 1 else behind[m + 1]
            steps_ref[m, pl.ds(0, C)] = jnp.where(group == 0, left, ahead[m]).astype(BF16)
            steps_ref[m, pl.ds(2 * C, C)] = jnp.where(group == F - 1, right, behind[m]).astype(BF16)
        total = product(ct_ref[...], jnp.concatenate([steps_ref[m] for m in range(count)], axis=1))
        streams, normed = [], []
        for m in range(count):
            stream = (near_ref[first + m].astype(F32) + total[:, LANES * m : LANES * (m + 1)]).astype(BF16)
            wide = stream.astype(F32)
            centred = wide - jnp.sum(wide, axis=0, keepdims=True) * (1.0 / C)
            spread = jnp.sum(centred * centred, axis=0, keepdims=True) * (1.0 / C)
            streams.append(stream)
            normed.append((centred * lax.rsqrt(spread + 1e-05)).astype(BF16))
        return streams, jnp.concatenate(normed, axis=1)

    streams, normed = temporal(2, F, edge_frame(1, team > 0, 0), edge_frame(2, team < teams - 1, F - 1))
    made = product(wqkv_ref[...], normed)
    for i in range(F):
        stream_ref[i] = streams[i]
        part = made[:, LANES * i : LANES * (i + 1)]
        for r in range(F):
            q_ref[r, i] = roll(part[:C], WIDE * r).astype(BF16)
            v_ref[r, 2 + i] = roll(part[2 * C :], -WIDE * r).astype(BF16)
        k_ref[2 + i] = part[C : 2 * C].astype(BF16)

    def keys(first, normed):
        made = product(wqkv_ref[pl.ds(C, 2 * C)], normed)
        for i in range(2):
            part = made[:, LANES * i : LANES * (i + 1)]
            k_ref[first + i] = part[:C].astype(BF16)
            for r in range(F):
                v_ref[r, first + i] = roll(part[C:], -WIDE * r).astype(BF16)

    head_row = lax.broadcasted_iota(jnp.int32, (8, LANES), 0)
    lane_frame = lax.shift_right_logical(lax.broadcasted_iota(jnp.int32, (8, LANES), 1), 5)
    reach_left = jnp.zeros((8, LANES), jnp.int32)
    reach_right = jnp.zeros((8, LANES), jnp.int32)
    for h in range(HEADS):
        reach_left = jnp.where(head_row == h, wl_ref[h], reach_left)
        reach_right = jnp.where(head_row == h, wr_ref[h], reach_right)
    summing = jnp.where(
        lax.shift_right_logical(lax.broadcasted_iota(jnp.int32, (16, C), 1), 6)
        == lax.broadcasted_iota(jnp.int32, (16, C), 0),
        1.0,
        0.0,
    ).astype(BF16)

    def attend(i, blocks, fresh):
        masked = []
        for m in blocks:
            products = jnp.concatenate([q_ref[r, i] * k_ref[m] for r in range(F)], axis=1)
            scores = product(summing, products)[:8] * HEAD_DIM ** (-0.5)
            for r in range(F):
                turned = roll(scores[:, LANES * r : LANES * (r + 1)], -WIDE * r)
                offset = F * (m - 2 - i) + jnp.bitwise_and(lane_frame + r, F - 1) - lane_frame
                allowed = (offset >= -reach_left) & (offset <= reach_right)
                masked.append(jnp.where(allowed, turned, -1e30))
        highest = functools.reduce(jnp.maximum, masked)
        if not fresh:
            before = m_ref[i]
            highest = jnp.maximum(highest, before)
            fade = jnp.exp(before - highest)
        raised = [jnp.exp(one - highest) for one in masked]
        total = functools.reduce(jnp.add, raised)
        if not fresh:
            total = total + l_ref[i] * fade
        m_ref[i] = highest
        l_ref[i] = total
        for h in range(HEADS):
            rows = pl.ds(HEAD_DIM * h, HEAD_DIM)
            acc = None if fresh else acc_ref[i, rows] * fade[h : h + 1]
            for n, m in enumerate(blocks):
                for r in range(F):
                    term = raised[F * n + r][h : h + 1] * v_ref[r, m, rows].astype(F32)
                    acc = term if acc is None else acc + term
            acc_ref[i, rows] = acc

    def loop(low, high, blocks, fresh):
        def step(i, carry):
            attend(i, blocks, fresh)
            return carry

        lax.fori_loop(low, high, step, 0)

    backs = {}

    def finish(pair):
        blended = []
        for i in pair:
            scale = 1.0 / l_ref[i]
            blended.append(
                jnp.concatenate(
                    [
                        (acc_ref[i, pl.ds(HEAD_DIM * h, HEAD_DIM)] * scale[h : h + 1]).astype(BF16)
                        for h in range(HEADS)
                    ],
                    axis=0,
                )
            )
        mixed = product(wo_ref[...], jnp.concatenate(blended, axis=1))
        for n, i in enumerate(pair):
            done = (stream_ref[i].astype(F32) + mixed[:, LANES * n : LANES * (n + 1)]).astype(BF16)
            done_ref[i] = done
            backs[i] = remote(
                done_ref.at[i], back_ref.at[mine], bs_sem.at[i], br_sem.at[mine], (F * team + i, ih)
            )

            @pl.when(mine != i)
            def _():
                backs[i].start()

            @pl.when(mine == i)
            def _():
                back_ref[mine] = done

    loop(0, F, (2, 3, 4, 5), True)

    @pl.when(team < teams - 1)
    def _():
        edge_arrived(3)
        halo_arrived(6)
        halo_arrived(7)
        before = roll(silu(near_ref[5].astype(F32)), WIDE)
        keys(6, temporal(6, 2, before, edge_frame(3, True, F - 1))[1])
        loop(2, 4, (6, 7), False)

    finish((2, 3))

    @pl.when(team > 0)
    def _():
        edge_arrived(0)
        halo_arrived(0)
        halo_arrived(1)
        after = roll(silu(near_ref[2].astype(F32)), -WIDE)
        keys(0, temporal(0, 2, edge_frame(0, True, 0), after)[1])
        loop(0, 2, (0, 1), False)

    finish((0, 1))

    for step in (1, 3, 2):
        member = lax.rem(mine + step, F)
        remote(
            done_ref.at[0], back_ref.at[member], bs_sem.at[0], br_sem.at[member], (it, h_next)
        ).wait_recv()
    lines = [back_ref[j].astype(F32) for j in range(F)]
    for f in range(F):
        whole = lines[0] if f == 0 else roll(lines[0], -WIDE * f)
        for j in range(1, F):
            whole = jnp.where(group == j, roll(lines[j], WIDE * (j - f)), whole)
        out_ref[f] = whole.astype(BF16)

    row_down.wait_send()
    row_up.wait_send()
    for j in range(F):

        @pl.when(mine != j)
        def _():
            swaps[j].wait_send()
            backs[j].wait_send()

        @pl.when(edge_wanted)
        def _():
            edges[j].wait_send()

    for late, copy in halos:

        @pl.when(wanted(late))
        def _():
            copy.wait_send()


def per_device(
    frames_in, conv_spatial, conv_temporal, w_query, w_key, w_value, w_out, win_left, win_right
):
    hbm = pl.BlockSpec(memory_space=pltpu.HBM)
    frame = (C, LANES)
    return pl.pallas_call(
        kernel,
        out_shape=jax.ShapeDtypeStruct(frames_in.shape, BF16),
        in_specs=[hbm] * 9,
        out_specs=pl.BlockSpec(memory_space=pltpu.VMEM),
        scratch_shapes=[
            pltpu.VMEM((F,) + frame, BF16),
            pltpu.VMEM((C, 9 * C), BF16),
            pltpu.VMEM((C, 3 * C), BF16),
            pltpu.VMEM((3 * C, C), BF16),
            pltpu.VMEM((C, C), BF16),
            pltpu.SMEM((HEADS,), jnp.int32),
            pltpu.SMEM((HEADS,), jnp.int32),
            pltpu.VMEM((F,) + frame, F32),
            pltpu.VMEM((F + 2, 3 * C, LANES), BF16),
            pltpu.VMEM((2,) + frame, BF16),
            pltpu.VMEM((F,) + frame, BF16),
            pltpu.VMEM((F, QUARTER, LANES), BF16),
            pltpu.VMEM((2 * F,) + frame, BF16),
            pltpu.VMEM((F, QUARTER, LANES), BF16),
            pltpu.VMEM((F, 3 * C, LANES), BF16),
            pltpu.VMEM((F,) + frame, BF16),
            pltpu.VMEM((F,) + frame, BF16),
            pltpu.VMEM((F,) + frame, BF16),
            pltpu.VMEM((F, F) + frame, BF16),
            pltpu.VMEM((2 * F,) + frame, BF16),
            pltpu.VMEM((F, 2 * F) + frame, BF16),
            pltpu.VMEM((F,) + frame, F32),
            pltpu.VMEM((F, 8, LANES), F32),
            pltpu.VMEM((F, 8, LANES), F32),
            pltpu.SemaphoreType.DMA((9,)),
            pltpu.SemaphoreType.DMA((2,)),
            pltpu.SemaphoreType.DMA((2,)),
            pltpu.SemaphoreType.DMA((F,)),
            pltpu.SemaphoreType.DMA((F,)),
            pltpu.SemaphoreType.DMA((F,)),
            pltpu.SemaphoreType.DMA((F,)),
            pltpu.SemaphoreType.DMA((F,)),
            pltpu.SemaphoreType.DMA((2 * F,)),
            pltpu.SemaphoreType.DMA((F,)),
            pltpu.SemaphoreType.DMA((F,)),
        ],
        compiler_params=pltpu.CompilerParams(
            collective_id=0, has_side_effects=True, vmem_limit_bytes=62 * 1024 * 1024
        ),
    )(win_left, win_right, frames_in, conv_spatial, conv_temporal, w_query, w_key, w_value, w_out)


def solution(mesh):
    return jax.shard_map(
        per_device,
        mesh=mesh,
        in_specs=(P("tm", None, "height"), P(), P(), P(), P(), P(), P(), P(), P()),
        out_specs=P("tm", None, "height"),
        check_vma=False,
    )
```

```python
import functools

import jax
import jax.numpy as jnp
from jax import lax
from jax.experimental import pallas as pl
from jax.experimental.pallas import tpu as pltpu
from jax.sharding import PartitionSpec as P

HEADS = 5
HEAD_DIM = 64
WIDE = 32
C = 320
F = 4
LANES = 128
QUARTER = C // F
MESH = pl.DeviceIdType.MESH
F32 = jnp.float32
BF16 = jnp.bfloat16


def silu(v):
    return 0.5 * v * (1.0 + jnp.tanh(0.5 * v))


def roll(v, shift):
    shift = shift % LANES
    return v if shift == 0 else pltpu.roll(v, shift, 1)


def kernel(
    wl_hbm,
    wr_hbm,
    x_hbm,
    cs_hbm,
    ct_hbm,
    wq_hbm,
    wk_hbm,
    wv_hbm,
    wo_hbm,
    out_ref,
    x_ref,
    cs_ref,
    ct_ref,
    wqkv_ref,
    wo_ref,
    wl_ref,
    wr_ref,
    rows_ref,
    taps_ref,
    above_ref,
    settled_ref,
    edge_ref,
    near_ref,
    far_ref,
    steps_ref,
    stream_ref,
    done_ref,
    back_ref,
    rim_ref,
    q_ref,
    k_ref,
    v_ref,
    acc_ref,
    m_ref,
    l_ref,
    load_sem,
    hs_sem,
    hr_sem,
    gs_sem,
    gr_sem,
    es_sem,
    er_sem,
    zs_sem,
    zr_sem,
    bs_sem,
    br_sem,
):
    nt = lax.axis_size("tm")
    nh = lax.axis_size("height")
    it = lax.axis_index("tm")
    ih = lax.axis_index("height")
    h_next, h_prev = lax.rem(ih + 1, nh), lax.rem(ih + nh - 1, nh)
    team, mine, teams = it // F, lax.rem(it, F), nt // F
    odd = lax.rem(mine, 2)
    later, earlier = lax.rem(team + 1, teams), lax.rem(team + teams - 1, teams)

    loads = []
    for n, (src, dst) in enumerate(
        (
            (x_hbm, x_ref),
            (cs_hbm, cs_ref),
            (ct_hbm, ct_ref),
            (wq_hbm, wqkv_ref.at[pl.ds(0, C)]),
            (wk_hbm, wqkv_ref.at[pl.ds(C, C)]),
            (wv_hbm, wqkv_ref.at[pl.ds(2 * C, C)]),
            (wo_hbm, wo_ref),
            (wl_hbm, wl_ref),
            (wr_hbm, wr_ref),
        )
    ):
        copy = pltpu.make_async_copy(src, dst, load_sem.at[n])
        copy.start()
        loads.append(copy)

    barrier = pltpu.get_barrier_semaphore()
    friends = [(it, h_next), (it, h_prev)]
    friends += [(F * team + lax.rem(mine + step, F), ih) for step in (1, 2, 3)]
    for dev in friends:
        pl.semaphore_signal(barrier, inc=1, device_id=dev, device_id_type=MESH)

    @pl.when(team > 0)
    def _():
        for dev in ((F * earlier + mine, ih), (F * earlier + 1, ih), (F * earlier + 3, ih)):
            pl.semaphore_signal(barrier, inc=1, device_id=dev, device_id_type=MESH)

    @pl.when(team < teams - 1)
    def _():
        for dev in ((F * later + mine, ih), (F * later, ih), (F * later + 2, ih)):
            pl.semaphore_signal(barrier, inc=1, device_id=dev, device_id_type=MESH)

    has_later, has_earlier = jnp.where(team < teams - 1, 1, 0), jnp.where(team > 0, 1, 0)
    greetings = len(friends) + has_later * (1 + F * odd) + has_earlier * (1 + F * (1 - odd))

    def remote(src, dst, ssem, rsem, dev):
        return pltpu.make_async_remote_copy(
            src_ref=src, dst_ref=dst, send_sem=ssem, recv_sem=rsem, device_id=dev, device_id_type=MESH
        )

    lane = lax.broadcasted_iota(jnp.int32, (C, LANES), 1)
    col = jnp.bitwise_and(lane, WIDE - 1)
    group = lax.shift_right_logical(lane, 5)
    block_group = lax.shift_right_logical(lax.broadcasted_iota(jnp.int32, (QUARTER, LANES), 1), 5)

    def fill(place, act):
        taps_ref[place, pl.ds(0, C)] = jnp.where(col == 0, 0.0, roll(act, 1)).astype(BF16)
        taps_ref[place, pl.ds(C, C)] = act.astype(BF16)
        taps_ref[place, pl.ds(2 * C, C)] = jnp.where(col == WIDE - 1, 0.0, roll(act, -1)).astype(BF16)

    loads[0].wait()
    frames = [x_ref[f].astype(F32) for f in range(F)]
    for j in range(F):
        row = jnp.zeros((C, LANES), F32)
        for f in range(F):
            row = jnp.where(group == f, roll(frames[f], WIDE * (f - j)), row)
        rows_ref[j] = row
        fill(j + 1, silu(row))

    pl.semaphore_wait(barrier, greetings)
    row_down = remote(
        taps_ref.at[F, pl.ds(C, C)], above_ref.at[0], hs_sem.at[0], hr_sem.at[0], (it, h_next)
    )
    row_up = remote(
        taps_ref.at[1, pl.ds(C, C)], above_ref.at[1], hs_sem.at[1], hr_sem.at[1], (it, h_prev)
    )
    row_down.start()
    row_up.start()

    def around(j):
        return taps_ref[pl.ds(j, 3)].reshape(9 * C, LANES)

    def product(weights, source):
        return jnp.dot(weights, source, preferred_element_type=F32)

    swaps, edges = {}, {}
    edge_team = jnp.where(odd == 1, later, earlier)
    edge_slot = jnp.where(odd == 1, 0, 2) + mine // 2
    edge_wanted = jnp.where(odd == 1, jnp.where(team < teams - 1, 1, 0), jnp.where(team > 0, 1, 0)) == 1

    def settle(j, spatial):
        settled = (rows_ref[j] + spatial).astype(BF16)
        settled_ref[j] = settled
        wide = settled.astype(F32)
        swaps[j] = remote(
            settled_ref.at[j], near_ref.at[2 + mine], gs_sem.at[j], gr_sem.at[mine], (F * team + j, ih)
        )

        @pl.when(mine != j)
        def _():
            swaps[j].start()

        @pl.when(mine == j)
        def _():
            near_ref[2 + j] = settled

        block = jnp.zeros((QUARTER, LANES), F32)
        for n in range(F):
            part = wide[QUARTER * n : QUARTER * (n + 1)]
            turned = jnp.where(odd == 1, roll(part, WIDE * (n + 1)), roll(part, WIDE * n))
            block = jnp.where(block_group == n, turned, block)
        edge_ref[j] = block.astype(BF16)
        edges[j] = remote(
            edge_ref.at[j], far_ref.at[edge_slot], es_sem.at[j], er_sem.at[edge_slot], (F * edge_team + j, ih)
        )

        @pl.when(edge_wanted)
        def _():
            edges[j].start()

    loads[1].wait()
    inner = product(cs_ref[...], jnp.concatenate([around(1), around(2)], axis=1))
    settle(1, inner[:, :LANES])
    settle(2, inner[:, LANES:])
    row_down.wait_recv()
    row_up.wait_recv()
    fill(0, jnp.where(ih > 0, above_ref[0].astype(F32), 0.0))
    fill(F + 1, jnp.where(ih < nh - 1, above_ref[1].astype(F32), 0.0))
    outer = product(cs_ref[...], jnp.concatenate([around(0), around(3)], axis=1))
    settle(0, outer[:, :LANES])
    settle(3, outer[:, LANES:])

    def swapped(member):
        return remote(
            settled_ref.at[0], near_ref.at[2 + member], gs_sem.at[0], gr_sem.at[member], (it, h_next)
        )

    def wanted(late):
        return jnp.where(late, jnp.where(team < teams - 1, 1, 0), jnp.where(team > 0, 1, 0)) == 1

    halos = []

    def send_halo(member):
        late = member >= 2
        place = jnp.where(late, member - 2, member + 6)
        copy = remote(
            near_ref.at[2 + member],
            near_ref.at[place],
            zs_sem.at[member],
            zr_sem.at[place],
            (F * jnp.where(late, later, earlier) + mine, ih),
        )
        halos.append((late, copy))

        @pl.when(wanted(late))
        def _():
            copy.start()

    send_halo(mine)
    for n in (2, 3, 4, 5, 6, 7, 8):
        loads[n].wait()
    for step in (1, 3, 2):
        member = lax.rem(mine + step, F)
        swapped(member).wait_recv()
        send_halo(member)

    def edge_arrived(slot):
        remote(edge_ref.at[0], far_ref.at[slot], es_sem.at[0], er_sem.at[slot], (it, h_next)).wait_recv()

    def halo_arrived(place):
        remote(near_ref.at[2], near_ref.at[place], zs_sem.at[0], zr_sem.at[place], (it, h_next)).wait_recv()

    @pl.when(team > 0)
    def _():
        edge_arrived(1)

    @pl.when(team < teams - 1)
    def _():
        edge_arrived(2)

    def edge_frame(slot, there, place):
        block = silu(jnp.where(there, far_ref[slot].astype(F32), 0.0))
        return jnp.concatenate([roll(block, WIDE * (place - n)) for n in range(F)], axis=0)

    def temporal(values, lefts, rights):
        ahead, behind = [], []
        for m in range(F):
            moving = silu(values[m])
            steps_ref[m, pl.ds(C, C)] = moving.astype(BF16)
            ahead.append(roll(moving, WIDE))
            behind.append(roll(moving, -WIDE))
        for m in range(F):
            left = ahead[m - 1] if lefts[m] is None else lefts[m]
            right = behind[m + 1] if rights[m] is None else rights[m]
            steps_ref[m, pl.ds(0, C)] = jnp.where(group == 0, left, ahead[m]).astype(BF16)
            steps_ref[m, pl.ds(2 * C, C)] = jnp.where(group == F - 1, right, behind[m]).astype(BF16)
        total = product(ct_ref[...], jnp.concatenate([steps_ref[m] for m in range(F)], axis=1))
        streams, normed = [], []
        for m in range(F):
            stream = (values[m] + total[:, LANES * m : LANES * (m + 1)]).astype(BF16)
            wide = stream.astype(F32)
            centred = wide - jnp.sum(wide, axis=0, keepdims=True) * (1.0 / C)
            spread = jnp.sum(centred * centred, axis=0, keepdims=True) * (1.0 / C)
            streams.append(stream)
            normed.append((centred * lax.rsqrt(spread + 1e-05)).astype(BF16))
        return streams, jnp.concatenate(normed, axis=1), behind[0], ahead[F - 1]

    streams, normed, first_frame, last_frame = temporal(
        [near_ref[2 + i].astype(F32) for i in range(F)],
        [edge_frame(1, team > 0, 0), None, None, None],
        [None, None, None, edge_frame(2, team < teams - 1, F - 1)],
    )
    rim_ref[0] = first_frame
    rim_ref[1] = last_frame
    made = product(wqkv_ref[...], normed)
    for i in range(F):
        stream_ref[i] = streams[i]
        part = made[:, LANES * i : LANES * (i + 1)]
        query, value = part[:C].astype(BF16), part[2 * C :].astype(BF16)
        for r in range(F):
            q_ref[r, i] = roll(query, WIDE * r)
            v_ref[r, 2 + i] = roll(value, -WIDE * r)
        k_ref[2 + i] = part[C : 2 * C].astype(BF16)

    head_row = lax.broadcasted_iota(jnp.int32, (8, LANES), 0)
    lane_frame = lax.shift_right_logical(lax.broadcasted_iota(jnp.int32, (8, LANES), 1), 5)
    reach_left = jnp.zeros((8, LANES), jnp.int32)
    reach_right = jnp.zeros((8, LANES), jnp.int32)
    for h in range(HEADS):
        reach_left = jnp.where(head_row == h, wl_ref[h], reach_left)
        reach_right = jnp.where(head_row == h, wr_ref[h], reach_right)
    summing = jnp.where(
        lax.shift_right_logical(lax.broadcasted_iota(jnp.int32, (16, C), 1), 6)
        == lax.broadcasted_iota(jnp.int32, (16, C), 0),
        1.0,
        0.0,
    ).astype(BF16)

    def attend(i, blocks, fresh, known=None):
        masked = []
        for m in blocks:
            products = jnp.concatenate([q_ref[r, i] * k_ref[m] for r in range(F)], axis=1)
            scores = product(summing, products)[:8] * HEAD_DIM ** (-0.5)
            for r in range(F):
                turned = roll(scores[:, LANES * r : LANES * (r + 1)], -WIDE * r)
                offset = F * (m - 2 - i) + jnp.bitwise_and(lane_frame + r, F - 1) - lane_frame
                if known is not None:
                    offset = jnp.where(known, offset, 2 * LANES)
                allowed = (offset >= -reach_left) & (offset <= reach_right)
                masked.append(jnp.where(allowed, turned, -1e30))
        highest = functools.reduce(jnp.maximum, masked)
        if not fresh:
            before = m_ref[i]
            highest = jnp.maximum(highest, before)
            fade = jnp.exp(before - highest)
        raised = [jnp.exp(one - highest) for one in masked]
        total = functools.reduce(jnp.add, raised)
        if not fresh:
            total = total + l_ref[i] * fade
        m_ref[i] = highest
        l_ref[i] = total
        for h in range(HEADS):
            rows = pl.ds(HEAD_DIM * h, HEAD_DIM)
            acc = None if fresh else acc_ref[i, rows] * fade[h : h + 1]
            for n, m in enumerate(blocks):
                for r in range(F):
                    term = raised[F * n + r][h : h + 1] * v_ref[r, m, rows].astype(F32)
                    acc = term if acc is None else acc + term
            acc_ref[i, rows] = acc

    def loop(low, high, blocks, fresh):
        def step(i, carry):
            attend(i, blocks, fresh)
            return carry

        lax.fori_loop(low, high, step, 0)

    backs = {}

    def finish(i):
        scale = 1.0 / l_ref[i]
        blended = jnp.concatenate(
            [
                (acc_ref[i, pl.ds(HEAD_DIM * h, HEAD_DIM)] * scale[h : h + 1]).astype(BF16)
                for h in range(HEADS)
            ],
            axis=0,
        )
        done = (stream_ref[i].astype(F32) + product(wo_ref[...], blended)).astype(BF16)
        done_ref[i] = done
        backs[i] = remote(
            done_ref.at[i], back_ref.at[mine], bs_sem.at[i], br_sem.at[mine], (F * team + i, ih)
        )

        @pl.when(mine != i)
        def _():
            backs[i].start()

        @pl.when(mine == i)
        def _():
            back_ref[mine] = done

    loop(0, F, (2, 3, 4, 5), True)

    @pl.when(team < teams - 1)
    def _():
        edge_arrived(3)
        halo_arrived(6)
        halo_arrived(7)

    @pl.when(team > 0)
    def _():
        edge_arrived(0)
        halo_arrived(0)
        halo_arrived(1)

    outside = (0, 1, 6, 7)
    there = (team > 0, team > 0, team < teams - 1, team < teams - 1)
    normed = temporal(
        [jnp.where(there[n], near_ref[outside[n]].astype(F32), 0.0) for n in range(F)],
        [edge_frame(0, team > 0, 0), None, rim_ref[1], None],
        [None, rim_ref[0], None, edge_frame(3, team < teams - 1, F - 1)],
    )[1]
    made = product(wqkv_ref[pl.ds(C, 2 * C)], normed)
    for n, m in enumerate(outside):
        part = made[:, LANES * n : LANES * (n + 1)].astype(BF16)
        k_ref[m] = part[:C]
        for r in range(F):
            v_ref[r, m] = roll(part[C:], -WIDE * r)
    for i, blocks, known in ((2, (6, 7), there[2]), (3, (6, 7), there[2]), (0, (0, 1), there[0]), (1, (0, 1), there[0])):
        attend(i, blocks, False, known)
        finish(i)

    for step in (1, 3, 2):
        member = lax.rem(mine + step, F)
        remote(
            done_ref.at[0], back_ref.at[member], bs_sem.at[0], br_sem.at[member], (it, h_next)
        ).wait_recv()
    lines = [back_ref[j].astype(F32) for j in range(F)]
    for f in range(F):
        whole = lines[0] if f == 0 else roll(lines[0], -WIDE * f)
        for j in range(1, F):
            whole = jnp.where(group == j, roll(lines[j], WIDE * (j - f)), whole)
        out_ref[f] = whole.astype(BF16)

    row_down.wait_send()
    row_up.wait_send()
    for j in range(F):

        @pl.when(mine != j)
        def _():
            swaps[j].wait_send()
            backs[j].wait_send()

        @pl.when(edge_wanted)
        def _():
            edges[j].wait_send()

    for late, copy in halos:

        @pl.when(wanted(late))
        def _():
            copy.wait_send()


def per_device(
    frames_in, conv_spatial, conv_temporal, w_query, w_key, w_value, w_out, win_left, win_right
):
    hbm = pl.BlockSpec(memory_space=pltpu.HBM)
    frame = (C, LANES)
    return pl.pallas_call(
        kernel,
        out_shape=jax.ShapeDtypeStruct(frames_in.shape, BF16),
        in_specs=[hbm] * 9,
        out_specs=pl.BlockSpec(memory_space=pltpu.VMEM),
        scratch_shapes=[
            pltpu.VMEM((F,) + frame, BF16),
            pltpu.VMEM((C, 9 * C), BF16),
            pltpu.VMEM((C, 3 * C), BF16),
            pltpu.VMEM((3 * C, C), BF16),
            pltpu.VMEM((C, C), BF16),
            pltpu.SMEM((HEADS,), jnp.int32),
            pltpu.SMEM((HEADS,), jnp.int32),
            pltpu.VMEM((F,) + frame, F32),
            pltpu.VMEM((F + 2, 3 * C, LANES), BF16),
            pltpu.VMEM((2,) + frame, BF16),
            pltpu.VMEM((F,) + frame, BF16),
            pltpu.VMEM((F, QUARTER, LANES), BF16),
            pltpu.VMEM((2 * F,) + frame, BF16),
            pltpu.VMEM((F, QUARTER, LANES), BF16),
            pltpu.VMEM((F, 3 * C, LANES), BF16),
            pltpu.VMEM((F,) + frame, BF16),
            pltpu.VMEM((F,) + frame, BF16),
            pltpu.VMEM((F,) + frame, BF16),
            pltpu.VMEM((2,) + frame, F32),
            pltpu.VMEM((F, F) + frame, BF16),
            pltpu.VMEM((2 * F,) + frame, BF16),
            pltpu.VMEM((F, 2 * F) + frame, BF16),
            pltpu.VMEM((F,) + frame, F32),
            pltpu.VMEM((F, 8, LANES), F32),
            pltpu.VMEM((F, 8, LANES), F32),
            pltpu.SemaphoreType.DMA((9,)),
            pltpu.SemaphoreType.DMA((2,)),
            pltpu.SemaphoreType.DMA((2,)),
            pltpu.SemaphoreType.DMA((F,)),
            pltpu.SemaphoreType.DMA((F,)),
            pltpu.SemaphoreType.DMA((F,)),
            pltpu.SemaphoreType.DMA((F,)),
            pltpu.SemaphoreType.DMA((F,)),
            pltpu.SemaphoreType.DMA((2 * F,)),
            pltpu.SemaphoreType.DMA((F,)),
            pltpu.SemaphoreType.DMA((F,)),
        ],
        compiler_params=pltpu.CompilerParams(
            collective_id=0, has_side_effects=True, vmem_limit_bytes=40 * 1024 * 1024
        ),
    )(
        *(
            pltpu.with_memory_space_constraint(v, pltpu.HBM)
            for v in (
                win_left,
                win_right,
                frames_in,
                conv_spatial,
                conv_temporal,
                w_query,
                w_key,
                w_value,
                w_out,
            )
        )
    )


def solution(mesh):
    return jax.shard_map(
        per_device,
        mesh=mesh,
        in_specs=(P("tm", None, "height"), P(), P(), P(), P(), P(), P(), P(), P()),
        out_specs=P("tm", None, "height"),
        check_vma=False,
    )
```

```python
import functools

import jax
import jax.numpy as jnp
from jax import lax
from jax.experimental import pallas as pl
from jax.experimental.pallas import tpu as pltpu
from jax.sharding import PartitionSpec as P

HEADS = 5
HEAD_DIM = 64
WIDE = 32
C = 320
F = 4
LANES = 128
QUARTER = C // F
COLUMN = 16
MESH = pl.DeviceIdType.MESH
F32 = jnp.float32
BF16 = jnp.bfloat16


def silu(v):
    return 0.5 * v * (1.0 + jnp.tanh(0.5 * v))


def roll(v, shift):
    shift = shift % LANES
    return v if shift == 0 else pltpu.roll(v, shift, 1)


def kernel(
    wl_hbm,
    wr_hbm,
    x_hbm,
    cs_hbm,
    ct_hbm,
    wq_hbm,
    wk_hbm,
    wv_hbm,
    wo_hbm,
    out_ref,
    x_ref,
    cs_ref,
    ct_ref,
    wqkv_ref,
    wo_ref,
    wl_ref,
    wr_ref,
    rows_ref,
    taps_ref,
    above_ref,
    settled_ref,
    edge_ref,
    near_ref,
    far_ref,
    steps_ref,
    stream_ref,
    done_ref,
    back_ref,
    rim_ref,
    q_ref,
    k_ref,
    v_ref,
    acc_ref,
    m_ref,
    l_ref,
    load_sem,
    hs_sem,
    hr_sem,
    gs_sem,
    gr_sem,
    es_sem,
    er_sem,
    zs_sem,
    zr_sem,
    bs_sem,
    br_sem,
    ok_sem,
):
    nt = lax.axis_size("tm")
    nh = lax.axis_size("height")
    it = lax.axis_index("tm")
    ih = lax.axis_index("height")
    h_next, h_prev = lax.rem(ih + 1, nh), lax.rem(ih + nh - 1, nh)
    team, mine, teams = it // F, lax.rem(it, F), nt // F
    odd = lax.rem(mine, 2)
    later, earlier = lax.rem(team + 1, teams), lax.rem(team + teams - 1, teams)

    loads = []
    for n, (src, dst) in enumerate(
        (
            (x_hbm, x_ref),
            (cs_hbm, cs_ref),
            (ct_hbm, ct_ref),
            (wq_hbm, wqkv_ref.at[pl.ds(0, C)]),
            (wk_hbm, wqkv_ref.at[pl.ds(C, C)]),
            (wv_hbm, wqkv_ref.at[pl.ds(2 * C, C)]),
            (wo_hbm, wo_ref),
            (wl_hbm, wl_ref),
            (wr_hbm, wr_ref),
        )
    ):
        copy = pltpu.make_async_copy(src, dst, load_sem.at[n])
        copy.start()
        loads.append(copy)

    barrier = pltpu.get_barrier_semaphore()
    friends = [(it, h_next), (it, h_prev)]
    friends += [(F * team + lax.rem(mine + step, F), ih) for step in (1, 2, 3)]
    for dev in friends:
        pl.semaphore_signal(barrier, inc=1, device_id=dev, device_id_type=MESH)

    @pl.when(team > 0)
    def _():
        for j in range(F):
            pl.semaphore_signal(barrier, inc=1, device_id=(F * earlier + j, ih), device_id_type=MESH)

    greetings = len(friends) + F * jnp.where(team < teams - 1, 1, 0)

    def remote(src, dst, ssem, rsem, dev):
        return pltpu.make_async_remote_copy(
            src_ref=src, dst_ref=dst, send_sem=ssem, recv_sem=rsem, device_id=dev, device_id_type=MESH
        )

    lane = lax.broadcasted_iota(jnp.int32, (C, LANES), 1)
    col = jnp.bitwise_and(lane, WIDE - 1)
    group = lax.shift_right_logical(lane, 5)
    block_group = lax.shift_right_logical(lax.broadcasted_iota(jnp.int32, (QUARTER, LANES), 1), 5)

    def fill(place, act):
        taps_ref[place, pl.ds(0, C)] = jnp.where(col == 0, 0.0, roll(act, 1)).astype(BF16)
        taps_ref[place, pl.ds(C, C)] = act.astype(BF16)
        taps_ref[place, pl.ds(2 * C, C)] = jnp.where(col == WIDE - 1, 0.0, roll(act, -1)).astype(BF16)

    loads[0].wait()
    frames = [x_ref[f].astype(F32) for f in range(F)]
    for j in range(F):
        row = jnp.zeros((C, LANES), F32)
        for f in range(F):
            row = jnp.where(group == f, roll(frames[f], WIDE * (f - j)), row)
        rows_ref[j] = row
        fill(j + 1, silu(row))

    pl.semaphore_wait(barrier, greetings)
    first = (team > 0) & (lax.rem(team, COLUMN) == 0)
    row_down = remote(
        taps_ref.at[F, pl.ds(C, C)], above_ref.at[0], hs_sem.at[0], hr_sem.at[0], (it, h_next)
    )
    row_up = remote(
        taps_ref.at[1, pl.ds(C, C)], above_ref.at[1], hs_sem.at[1], hr_sem.at[1], (it, h_prev)
    )

    @pl.when(ih < nh - 1)
    def _():
        row_down.start()

    @pl.when(ih > 0)
    def _():
        row_up.start()

    @pl.when(team < teams - 1)
    def _():
        for j in range(F):
            pl.semaphore_signal(ok_sem, inc=1, device_id=(F * later + j, ih), device_id_type=MESH)


    def around(j):
        return taps_ref[pl.ds(j, 3)].reshape(9 * C, LANES)

    def product(weights, source):
        return jnp.dot(weights, source, preferred_element_type=F32)

    swaps, edges = {}, {}
    edge_team = jnp.where(odd == 1, later, earlier)
    edge_slot = jnp.where(odd == 1, 0, 2) + mine // 2
    edge_wanted = jnp.where(odd == 1, jnp.where(team < teams - 1, 1, 0), jnp.where(team > 0, 1, 0)) == 1

    def settle(j, spatial):
        settled = (rows_ref[j] + spatial).astype(BF16)
        settled_ref[j] = settled
        wide = settled.astype(F32)
        swaps[j] = remote(
            settled_ref.at[j], near_ref.at[2 + mine], gs_sem.at[j], gr_sem.at[mine], (F * team + j, ih)
        )

        @pl.when(mine != j)
        def _():
            swaps[j].start()

        @pl.when(mine == j)
        def _():
            near_ref[2 + j] = settled

        block = jnp.zeros((QUARTER, LANES), F32)
        for n in range(F):
            part = wide[QUARTER * n : QUARTER * (n + 1)]
            turned = jnp.where(odd == 1, roll(part, WIDE * (n + 1)), roll(part, WIDE * n))
            block = jnp.where(block_group == n, turned, block)
        edge_ref[j] = block.astype(BF16)
        edges[j] = remote(
            edge_ref.at[j], far_ref.at[edge_slot], es_sem.at[j], er_sem.at[edge_slot], (F * edge_team + j, ih)
        )

        @pl.when((odd == 1) & (team < teams - 1))
        def _():
            edges[j].start()

    loads[1].wait()
    inner = product(cs_ref[...], jnp.concatenate([around(1), around(2)], axis=1))
    settle(1, inner[:, :LANES])
    settle(2, inner[:, LANES:])

    @pl.when(ih > 0)
    def _():
        row_down.wait_recv()

    @pl.when(ih < nh - 1)
    def _():
        row_up.wait_recv()

    fill(0, jnp.where(ih > 0, above_ref[0].astype(F32), 0.0))
    fill(F + 1, jnp.where(ih < nh - 1, above_ref[1].astype(F32), 0.0))
    outer = product(cs_ref[...], jnp.concatenate([around(0), around(3)], axis=1))
    settle(0, outer[:, :LANES])
    settle(3, outer[:, LANES:])

    def open_earlier():
        pl.semaphore_wait(ok_sem, F)

        @pl.when(odd == 0)
        def _():
            for j in range(F):
                edges[j].start()

    @pl.when((team > 0) & jnp.logical_not(first))
    def _():
        open_earlier()

    def swapped(member):
        return remote(
            settled_ref.at[0], near_ref.at[2 + member], gs_sem.at[0], gr_sem.at[member], (it, h_next)
        )

    def wanted(late):
        return jnp.where(late, jnp.where(team < teams - 1, 1, 0), jnp.where(team > 0, 1, 0)) == 1

    halos = []

    def send_halo(member):
        late = member >= 2
        place = jnp.where(late, member - 2, member + 6)
        copy = remote(
            near_ref.at[2 + member],
            near_ref.at[place],
            zs_sem.at[member],
            zr_sem.at[place],
            (F * jnp.where(late, later, earlier) + mine, ih),
        )
        halos.append((late, copy))

        @pl.when(wanted(late) & (late | jnp.logical_not(first)))
        def _():
            copy.start()

    send_halo(mine)
    for n in (2, 3, 4, 5, 6, 7, 8):
        loads[n].wait()
    for step in (1, 3, 2):
        member = lax.rem(mine + step, F)
        swapped(member).wait_recv()
        send_halo(member)

    @pl.when(first)
    def _():
        open_earlier()
        for m in (0, 1):
            remote(
                near_ref.at[2 + m],
                near_ref.at[6 + m],
                zs_sem.at[m],
                zr_sem.at[6 + m],
                (F * earlier + mine, ih),
            ).start()

    def edge_arrived(slot):
        remote(edge_ref.at[0], far_ref.at[slot], es_sem.at[0], er_sem.at[slot], (it, h_next)).wait_recv()

    def halo_arrived(place):
        remote(near_ref.at[2], near_ref.at[place], zs_sem.at[0], zr_sem.at[place], (it, h_next)).wait_recv()

    @pl.when(team > 0)
    def _():
        edge_arrived(1)

    @pl.when(team < teams - 1)
    def _():
        edge_arrived(2)

    def edge_frame(slot, there, place):
        block = silu(jnp.where(there, far_ref[slot].astype(F32), 0.0))
        return jnp.concatenate([roll(block, WIDE * (place - n)) for n in range(F)], axis=0)

    def temporal(values, lefts, rights):
        count = len(values)
        ahead, behind = [], []
        for m in range(count):
            moving = silu(values[m])
            steps_ref[m, pl.ds(C, C)] = moving.astype(BF16)
            ahead.append(roll(moving, WIDE))
            behind.append(roll(moving, -WIDE))
        for m in range(count):
            left = ahead[m - 1] if lefts[m] is None else lefts[m]
            right = behind[m + 1] if rights[m] is None else rights[m]
            steps_ref[m, pl.ds(0, C)] = jnp.where(group == 0, left, ahead[m]).astype(BF16)
            steps_ref[m, pl.ds(2 * C, C)] = jnp.where(group == F - 1, right, behind[m]).astype(BF16)
        total = product(ct_ref[...], jnp.concatenate([steps_ref[m] for m in range(count)], axis=1))
        streams, normed = [], []
        for m in range(count):
            stream = (values[m] + total[:, LANES * m : LANES * (m + 1)]).astype(BF16)
            wide = stream.astype(F32)
            centred = wide - jnp.sum(wide, axis=0, keepdims=True) * (1.0 / C)
            spread = jnp.sum(centred * centred, axis=0, keepdims=True) * (1.0 / C)
            streams.append(stream)
            normed.append((centred * lax.rsqrt(spread + 1e-05)).astype(BF16))
        return streams, jnp.concatenate(normed, axis=1), behind[0], ahead[count - 1]

    streams, normed, first_frame, last_frame = temporal(
        [near_ref[2 + i].astype(F32) for i in range(F)],
        [edge_frame(1, team > 0, 0), None, None, None],
        [None, None, None, edge_frame(2, team < teams - 1, F - 1)],
    )
    rim_ref[0] = first_frame
    rim_ref[1] = last_frame
    made = product(wqkv_ref[...], normed)
    for i in range(F):
        stream_ref[i] = streams[i]
        part = made[:, LANES * i : LANES * (i + 1)]
        query, value = part[:C].astype(BF16), part[2 * C :].astype(BF16)
        for r in range(F):
            q_ref[r, i] = roll(query, WIDE * r)
            v_ref[r, 2 + i] = roll(value, -WIDE * r)
        k_ref[2 + i] = part[C : 2 * C].astype(BF16)

    head_row = lax.broadcasted_iota(jnp.int32, (8, LANES), 0)
    lane_frame = lax.shift_right_logical(lax.broadcasted_iota(jnp.int32, (8, LANES), 1), 5)
    reach_left = jnp.zeros((8, LANES), jnp.int32)
    reach_right = jnp.zeros((8, LANES), jnp.int32)
    for h in range(HEADS):
        reach_left = jnp.where(head_row == h, wl_ref[h], reach_left)
        reach_right = jnp.where(head_row == h, wr_ref[h], reach_right)
    summing = jnp.where(
        lax.shift_right_logical(lax.broadcasted_iota(jnp.int32, (16, C), 1), 6)
        == lax.broadcasted_iota(jnp.int32, (16, C), 0),
        1.0,
        0.0,
    ).astype(BF16)

    def attend(i, blocks, fresh, known=None):
        masked = []
        for m in blocks:
            products = jnp.concatenate([q_ref[r, i] * k_ref[m] for r in range(F)], axis=1)
            scores = product(summing, products)[:8] * HEAD_DIM ** (-0.5)
            for r in range(F):
                turned = roll(scores[:, LANES * r : LANES * (r + 1)], -WIDE * r)
                offset = F * (m - 2 - i) + jnp.bitwise_and(lane_frame + r, F - 1) - lane_frame
                if known is not None:
                    offset = jnp.where(known, offset, 2 * LANES)
                allowed = (offset >= -reach_left) & (offset <= reach_right)
                masked.append(jnp.where(allowed, turned, -1e30))
        highest = functools.reduce(jnp.maximum, masked)
        if not fresh:
            before = m_ref[i]
            highest = jnp.maximum(highest, before)
            fade = jnp.exp(before - highest)
        raised = [jnp.exp(one - highest) for one in masked]
        total = functools.reduce(jnp.add, raised)
        if not fresh:
            total = total + l_ref[i] * fade
        m_ref[i] = highest
        l_ref[i] = total
        for h in range(HEADS):
            rows = pl.ds(HEAD_DIM * h, HEAD_DIM)
            acc = None if fresh else acc_ref[i, rows] * fade[h : h + 1]
            for n, m in enumerate(blocks):
                for r in range(F):
                    term = raised[F * n + r][h : h + 1] * v_ref[r, m, rows].astype(F32)
                    acc = term if acc is None else acc + term
            acc_ref[i, rows] = acc

    def loop(low, high, blocks, fresh):
        def step(i, carry):
            attend(i, blocks, fresh)
            return carry

        lax.fori_loop(low, high, step, 0)

    backs = {}

    def finish(pair):
        blended = []
        for i in pair:
            scale = 1.0 / l_ref[i]
            blended.append(
                jnp.concatenate(
                    [
                        (acc_ref[i, pl.ds(HEAD_DIM * h, HEAD_DIM)] * scale[h : h + 1]).astype(BF16)
                        for h in range(HEADS)
                    ],
                    axis=0,
                )
            )
        mixed = product(wo_ref[...], jnp.concatenate(blended, axis=1))
        for n, i in enumerate(pair):
            done_ref[i] = (stream_ref[i].astype(F32) + mixed[:, LANES * n : LANES * (n + 1)]).astype(BF16)
        for i in pair:
            backs[i] = remote(
                done_ref.at[i], back_ref.at[mine], bs_sem.at[i], br_sem.at[mine], (F * team + i, ih)
            )

            @pl.when(mine != i)
            def _():
                backs[i].start()

            @pl.when(mine == i)
            def _():
                back_ref[mine] = done_ref[i]

    loop(0, F, (2, 3, 4, 5), True)

    def side(places, edge, known, lefts, rights, pair):
        @pl.when(known)
        def _():
            edge_arrived(edge)
            for place in places:
                halo_arrived(place)

        values = [jnp.where(known, near_ref[place].astype(F32), 0.0) for place in places]
        normed = temporal(values, lefts(), rights())[1]
        made = product(wqkv_ref[pl.ds(C, 2 * C)], normed)
        for n, place in enumerate(places):
            part = made[:, LANES * n : LANES * (n + 1)].astype(BF16)
            k_ref[place] = part[:C]
            for r in range(F):
                v_ref[r, place] = roll(part[C:], -WIDE * r)
        for i in pair:
            attend(i, places, False, known)
        finish(pair)

    side(
        (6, 7),
        3,
        team < teams - 1,
        lambda: [rim_ref[1], None],
        lambda: [None, edge_frame(3, team < teams - 1, F - 1)],
        (2, 3),
    )
    side(
        (0, 1),
        0,
        team > 0,
        lambda: [edge_frame(0, team > 0, 0), None],
        lambda: [None, rim_ref[0]],
        (0, 1),
    )

    for step in (1, 3, 2):
        member = lax.rem(mine + step, F)
        remote(
            done_ref.at[0], back_ref.at[member], bs_sem.at[0], br_sem.at[member], (it, h_next)
        ).wait_recv()
    lines = [back_ref[j].astype(F32) for j in range(F)]
    for f in range(F):
        whole = lines[0] if f == 0 else roll(lines[0], -WIDE * f)
        for j in range(1, F):
            whole = jnp.where(group == j, roll(lines[j], WIDE * (j - f)), whole)
        out_ref[f] = whole.astype(BF16)

    @pl.when(ih < nh - 1)
    def _():
        row_down.wait_send()

    @pl.when(ih > 0)
    def _():
        row_up.wait_send()

    for j in range(F):

        @pl.when(mine != j)
        def _():
            swaps[j].wait_send()
            backs[j].wait_send()

        @pl.when(edge_wanted)
        def _():
            edges[j].wait_send()

    for late, copy in halos:

        @pl.when(wanted(late))
        def _():
            copy.wait_send()


def per_device(
    frames_in, conv_spatial, conv_temporal, w_query, w_key, w_value, w_out, win_left, win_right
):
    hbm = pl.BlockSpec(memory_space=pltpu.HBM)
    frame = (C, LANES)
    return pl.pallas_call(
        kernel,
        out_shape=jax.ShapeDtypeStruct(frames_in.shape, BF16),
        in_specs=[hbm] * 9,
        out_specs=pl.BlockSpec(memory_space=pltpu.VMEM),
        scratch_shapes=[
            pltpu.VMEM((F,) + frame, BF16),
            pltpu.VMEM((C, 9 * C), BF16),
            pltpu.VMEM((C, 3 * C), BF16),
            pltpu.VMEM((3 * C, C), BF16),
            pltpu.VMEM((C, C), BF16),
            pltpu.SMEM((HEADS,), jnp.int32),
            pltpu.SMEM((HEADS,), jnp.int32),
            pltpu.VMEM((F,) + frame, F32),
            pltpu.VMEM((F + 2, 3 * C, LANES), BF16),
            pltpu.VMEM((2,) + frame, BF16),
            pltpu.VMEM((F,) + frame, BF16),
            pltpu.VMEM((F, QUARTER, LANES), BF16),
            pltpu.VMEM((2 * F,) + frame, BF16),
            pltpu.VMEM((F, QUARTER, LANES), BF16),
            pltpu.VMEM((F, 3 * C, LANES), BF16),
            pltpu.VMEM((F,) + frame, BF16),
            pltpu.VMEM((F,) + frame, BF16),
            pltpu.VMEM((F,) + frame, BF16),
            pltpu.VMEM((2,) + frame, F32),
            pltpu.VMEM((F, F) + frame, BF16),
            pltpu.VMEM((2 * F,) + frame, BF16),
            pltpu.VMEM((F, 2 * F) + frame, BF16),
            pltpu.VMEM((F,) + frame, F32),
            pltpu.VMEM((F, 8, LANES), F32),
            pltpu.VMEM((F, 8, LANES), F32),
            pltpu.SemaphoreType.DMA((9,)),
            pltpu.SemaphoreType.DMA((2,)),
            pltpu.SemaphoreType.DMA((2,)),
            pltpu.SemaphoreType.DMA((F,)),
            pltpu.SemaphoreType.DMA((F,)),
            pltpu.SemaphoreType.DMA((F,)),
            pltpu.SemaphoreType.DMA((F,)),
            pltpu.SemaphoreType.DMA((F,)),
            pltpu.SemaphoreType.DMA((2 * F,)),
            pltpu.SemaphoreType.DMA((F,)),
            pltpu.SemaphoreType.DMA((F,)),
            pltpu.SemaphoreType.REGULAR,
        ],
        compiler_params=pltpu.CompilerParams(
            collective_id=0, has_side_effects=True, vmem_limit_bytes=40 * 1024 * 1024
        ),
    )(
        *(
            pltpu.with_memory_space_constraint(v, pltpu.HBM)
            for v in (
                win_left,
                win_right,
                frames_in,
                conv_spatial,
                conv_temporal,
                w_query,
                w_key,
                w_value,
                w_out,
            )
        )
    )


def solution(mesh):
    return jax.shard_map(
        per_device,
        mesh=mesh,
        in_specs=(P("tm", None, "height"), P(), P(), P(), P(), P(), P(), P(), P()),
        out_specs=P("tm", None, "height"),
        check_vma=False,
    )
```

```python
import functools

import jax
import jax.numpy as jnp
from jax import lax
from jax.experimental import pallas as pl
from jax.experimental.pallas import tpu as pltpu
from jax.sharding import PartitionSpec as P

HEADS = 5
HEAD_DIM = 64
WIDE = 32
C = 320
F = 4
LANES = 128
QUARTER = C // F
COLUMN = 16
MESH = pl.DeviceIdType.MESH
F32 = jnp.float32
BF16 = jnp.bfloat16


def silu(v):
    return 0.5 * v * (1.0 + jnp.tanh(0.5 * v))


def roll(v, shift):
    shift = shift % LANES
    return v if shift == 0 else pltpu.roll(v, shift, 1)


def kernel(
    wl_hbm,
    wr_hbm,
    x_hbm,
    cs_hbm,
    ct_hbm,
    wq_hbm,
    wk_hbm,
    wv_hbm,
    wo_hbm,
    out_ref,
    x_ref,
    cs_ref,
    ct_ref,
    wqkv_ref,
    wo_ref,
    wl_ref,
    wr_ref,
    rows_ref,
    taps_ref,
    above_ref,
    settled_ref,
    edge_ref,
    near_ref,
    far_ref,
    steps_ref,
    stream_ref,
    done_ref,
    back_ref,
    rim_ref,
    q_ref,
    k_ref,
    v_ref,
    acc_ref,
    m_ref,
    l_ref,
    load_sem,
    hs_sem,
    hr_sem,
    gs_sem,
    gr_sem,
    es_sem,
    er_sem,
    zs_sem,
    zr_sem,
    bs_sem,
    br_sem,
    ds_sem,
    ok_sem,
):
    nt = lax.axis_size("tm")
    nh = lax.axis_size("height")
    it = lax.axis_index("tm")
    ih = lax.axis_index("height")
    h_next, h_prev = lax.rem(ih + 1, nh), lax.rem(ih + nh - 1, nh)
    team, mine, teams = it // F, lax.rem(it, F), nt // F
    odd = lax.rem(mine, 2)
    later, earlier = lax.rem(team + 1, teams), lax.rem(team + teams - 1, teams)

    loads = []
    for n, (src, dst) in enumerate(
        (
            (x_hbm, x_ref),
            (cs_hbm, cs_ref),
            (ct_hbm, ct_ref),
            (wq_hbm, wqkv_ref.at[pl.ds(0, C)]),
            (wk_hbm, wqkv_ref.at[pl.ds(C, C)]),
            (wv_hbm, wqkv_ref.at[pl.ds(2 * C, C)]),
            (wo_hbm, wo_ref),
            (wl_hbm, wl_ref),
            (wr_hbm, wr_ref),
        )
    ):
        copy = pltpu.make_async_copy(src, dst, load_sem.at[n])
        copy.start()
        loads.append(copy)

    barrier = pltpu.get_barrier_semaphore()
    friends = [(it, h_next), (it, h_prev)]
    friends += [(F * team + lax.rem(mine + step, F), ih) for step in (1, 2, 3)]
    for dev in friends:
        pl.semaphore_signal(barrier, inc=1, device_id=dev, device_id_type=MESH)

    @pl.when(team > 0)
    def _():
        for j in range(F):
            pl.semaphore_signal(barrier, inc=1, device_id=(F * earlier + j, ih), device_id_type=MESH)

    greetings = len(friends) + F * jnp.where(team < teams - 1, 1, 0)

    def remote(src, dst, ssem, rsem, dev):
        return pltpu.make_async_remote_copy(
            src_ref=src, dst_ref=dst, send_sem=ssem, recv_sem=rsem, device_id=dev, device_id_type=MESH
        )

    lane = lax.broadcasted_iota(jnp.int32, (C, LANES), 1)
    col = jnp.bitwise_and(lane, WIDE - 1)
    group = lax.shift_right_logical(lane, 5)
    block_group = lax.shift_right_logical(lax.broadcasted_iota(jnp.int32, (QUARTER, LANES), 1), 5)

    def fill(place, act):
        taps_ref[place, pl.ds(0, C)] = jnp.where(col == 0, 0.0, roll(act, 1)).astype(BF16)
        taps_ref[place, pl.ds(C, C)] = act.astype(BF16)
        taps_ref[place, pl.ds(2 * C, C)] = jnp.where(col == WIDE - 1, 0.0, roll(act, -1)).astype(BF16)

    loads[0].wait()
    frames = [x_ref[f].astype(F32) for f in range(F)]
    for j in range(F):
        row = jnp.zeros((C, LANES), F32)
        for f in range(F):
            row = jnp.where(group == f, roll(frames[f], WIDE * (f - j)), row)
        rows_ref[j] = row
        fill(j + 1, silu(row))

    pl.semaphore_wait(barrier, greetings)
    first = (team > 0) & (lax.rem(team, COLUMN) == 0)
    direct = (team < teams - 1) & (lax.rem(team, COLUMN) == COLUMN - 1)
    outer_row = jnp.where(mine == 0, 1, jnp.where(mine == F - 1, 1, 0))
    straight = {}
    row_down = remote(
        taps_ref.at[F, pl.ds(C, C)], above_ref.at[0], hs_sem.at[0], hr_sem.at[0], (it, h_next)
    )
    row_up = remote(
        taps_ref.at[1, pl.ds(C, C)], above_ref.at[1], hs_sem.at[1], hr_sem.at[1], (it, h_prev)
    )

    @pl.when(ih < nh - 1)
    def _():
        row_down.start()

    @pl.when(ih > 0)
    def _():
        row_up.start()

    @pl.when(team < teams - 1)
    def _():
        for j in range(F):
            pl.semaphore_signal(ok_sem, inc=1, device_id=(F * later + j, ih), device_id_type=MESH)


    def around(j):
        return taps_ref[pl.ds(j, 3)].reshape(9 * C, LANES)

    def product(weights, source):
        return jnp.dot(weights, source, preferred_element_type=F32)

    swaps, edges = {}, {}
    edge_team = jnp.where(odd == 1, later, earlier)
    edge_slot = jnp.where(odd == 1, 0, 2) + mine // 2
    edge_wanted = jnp.where(odd == 1, jnp.where(team < teams - 1, 1, 0), jnp.where(team > 0, 1, 0)) == 1

    def settle(j, spatial):
        settled = (rows_ref[j] + spatial).astype(BF16)
        settled_ref[j] = settled
        wide = settled.astype(F32)
        block = jnp.zeros((QUARTER, LANES), F32)
        for n in range(F):
            part = wide[QUARTER * n : QUARTER * (n + 1)]
            turned = jnp.where(odd == 1, roll(part, WIDE * (n + 1)), roll(part, WIDE * n))
            block = jnp.where(block_group == n, turned, block)
        edge_ref[j] = block.astype(BF16)
        edges[j] = remote(
            edge_ref.at[j], far_ref.at[edge_slot], es_sem.at[j], er_sem.at[edge_slot], (F * edge_team + j, ih)
        )

        @pl.when((odd == 1) & (team < teams - 1))
        def _():
            edges[j].start()

        swaps[j] = remote(
            settled_ref.at[j], near_ref.at[2 + mine], gs_sem.at[j], gr_sem.at[mine], (F * team + j, ih)
        )

        if j in (0, F - 1):
            place = jnp.maximum(mine - 2, 0)
            straight[j] = remote(
                settled_ref.at[j], near_ref.at[place], ds_sem.at[j], zr_sem.at[place], (F * later + j, ih)
            )

            @pl.when(direct & (mine >= 2))
            def _():
                straight[j].start()

        @pl.when(mine != j)
        def _():
            swaps[j].start()

        @pl.when(mine == j)
        def _():
            near_ref[2 + j] = settled

    loads[1].wait()
    inner = product(cs_ref[...], jnp.concatenate([around(1), around(2)], axis=1))
    settle(1, inner[:, :LANES])
    settle(2, inner[:, LANES:])
    middle = product(
        cs_ref[:, 1024:1920],
        jnp.concatenate([taps_ref[1, pl.ds(64, 896)], taps_ref[F, pl.ds(64, 896)]], axis=1),
    )

    @pl.when(ih > 0)
    def _():
        row_down.wait_recv()

    @pl.when(ih < nh - 1)
    def _():
        row_up.wait_recv()

    fill(0, jnp.where(ih > 0, above_ref[0].astype(F32), 0.0))
    fill(F + 1, jnp.where(ih < nh - 1, above_ref[1].astype(F32), 0.0))
    outer = product(
        cs_ref[:, 0:1024], jnp.concatenate([around(0)[0:1024], around(3)[0:1024]], axis=1)
    )
    outer += product(
        cs_ref[:, 1920:2880], jnp.concatenate([taps_ref[2], taps_ref[F + 1]], axis=1)
    )
    outer += middle
    settle(0, outer[:, :LANES])
    settle(3, outer[:, LANES:])

    def open_earlier():
        pl.semaphore_wait(ok_sem, F)

        @pl.when(odd == 0)
        def _():
            for j in range(F):
                edges[j].start()

    @pl.when((team > 0) & jnp.logical_not(first))
    def _():
        open_earlier()

    def swapped(member):
        return remote(
            settled_ref.at[0], near_ref.at[2 + member], gs_sem.at[0], gr_sem.at[member], (it, h_next)
        )

    def wanted(late):
        return jnp.where(late, jnp.where(team < teams - 1, 1, 0), jnp.where(team > 0, 1, 0)) == 1

    halos = []

    def send_halo(member):
        late = member >= 2
        place = jnp.where(late, member - 2, member + 6)
        copy = remote(
            near_ref.at[2 + member],
            near_ref.at[place],
            zs_sem.at[member],
            zr_sem.at[place],
            (F * jnp.where(late, later, earlier) + mine, ih),
        )
        sent = wanted(late) & jnp.logical_not(late & direct & (outer_row == 1))
        halos.append((sent, copy))

        @pl.when(sent & (late | jnp.logical_not(first)))
        def _():
            copy.start()

    send_halo(mine)
    for n in (2, 3, 4, 5, 6, 7, 8):
        loads[n].wait()
    for step in (1, 3, 2):
        member = lax.rem(mine + step, F)
        swapped(member).wait_recv()
        send_halo(member)

    def edge_arrived(slot):
        remote(edge_ref.at[0], far_ref.at[slot], es_sem.at[0], er_sem.at[slot], (it, h_next)).wait_recv()

    def halo_arrived(place):
        remote(near_ref.at[2], near_ref.at[place], zs_sem.at[0], zr_sem.at[place], (it, h_next)).wait_recv()

    def edge_frame(slot, there, place):
        block = silu(jnp.where(there, far_ref[slot].astype(F32), 0.0))
        return jnp.concatenate([roll(block, WIDE * (place - n)) for n in range(F)], axis=0)

    def temporal(values, lefts, rights):
        count = len(values)
        ahead, behind = [], []
        for m in range(count):
            moving = silu(values[m])
            steps_ref[m, pl.ds(C, C)] = moving.astype(BF16)
            ahead.append(roll(moving, WIDE))
            behind.append(roll(moving, -WIDE))
        for m in range(count):
            left = ahead[m - 1] if lefts[m] is None else lefts[m]
            right = behind[m + 1] if rights[m] is None else rights[m]
            steps_ref[m, pl.ds(0, C)] = jnp.where(group == 0, left, ahead[m]).astype(BF16)
            steps_ref[m, pl.ds(2 * C, C)] = jnp.where(group == F - 1, right, behind[m]).astype(BF16)
        total = product(ct_ref[...], jnp.concatenate([steps_ref[m] for m in range(count)], axis=1))
        streams, normed = [], []
        for m in range(count):
            stream = (values[m] + total[:, LANES * m : LANES * (m + 1)]).astype(BF16)
            wide = stream.astype(F32)
            centred = wide - jnp.sum(wide, axis=0, keepdims=True) * (1.0 / C)
            spread = jnp.sum(centred * centred, axis=0, keepdims=True) * (1.0 / C)
            streams.append(stream)
            normed.append((centred * lax.rsqrt(spread + 1e-05)).astype(BF16))
        return streams, jnp.concatenate(normed, axis=1), behind[0]

    def side_keys(places, edge, lefts, rights):
        edge_arrived(edge)
        for place in places:
            halo_arrived(place)
        normed = temporal([near_ref[place].astype(F32) for place in places], lefts(), rights())[1]
        made = product(wqkv_ref[pl.ds(C, 2 * C)], normed)
        for n, place in enumerate(places):
            part = made[:, LANES * n : LANES * (n + 1)].astype(BF16)
            k_ref[place] = part[:C]
            for r in range(F):
                v_ref[r, place] = roll(part[C:], -WIDE * r)

    def next_keys():
        side_keys(
            (6, 7),
            3,
            lambda: [roll(silu(near_ref[5].astype(F32)), WIDE), None],
            lambda: [None, edge_frame(3, True, F - 1)],
        )

    head_row = lax.broadcasted_iota(jnp.int32, (8, LANES), 0)
    lane_frame = lax.shift_right_logical(lax.broadcasted_iota(jnp.int32, (8, LANES), 1), 5)
    reach_left = jnp.zeros((8, LANES), jnp.int32)
    reach_right = jnp.zeros((8, LANES), jnp.int32)
    for h in range(HEADS):
        reach_left = jnp.where(head_row == h, wl_ref[h], reach_left)
        reach_right = jnp.where(head_row == h, wr_ref[h], reach_right)
    summing = jnp.where(
        lax.shift_right_logical(lax.broadcasted_iota(jnp.int32, (16, C), 1), 6)
        == lax.broadcasted_iota(jnp.int32, (16, C), 0),
        1.0,
        0.0,
    ).astype(BF16)

    def attend(i, blocks, fresh):
        masked = []
        for m in blocks:
            products = jnp.concatenate([q_ref[r, i] * k_ref[m] for r in range(F)], axis=1)
            scores = product(summing, products)[:8] * HEAD_DIM ** (-0.5)
            for r in range(F):
                turned = roll(scores[:, LANES * r : LANES * (r + 1)], -WIDE * r)
                offset = F * (m - 2 - i) + jnp.bitwise_and(lane_frame + r, F - 1) - lane_frame
                allowed = (offset >= -reach_left) & (offset <= reach_right)
                masked.append(jnp.where(allowed, turned, -1e30))
        highest = functools.reduce(jnp.maximum, masked)
        if not fresh:
            before = m_ref[i]
            highest = jnp.maximum(highest, before)
            fade = jnp.exp(before - highest)
        raised = [jnp.exp(one - highest) for one in masked]
        total = functools.reduce(jnp.add, raised)
        if not fresh:
            total = total + l_ref[i] * fade
        m_ref[i] = highest
        l_ref[i] = total
        for h in range(HEADS):
            rows = pl.ds(HEAD_DIM * h, HEAD_DIM)
            acc = None if fresh else acc_ref[i, rows] * fade[h : h + 1]
            for n, m in enumerate(blocks):
                for r in range(F):
                    term = raised[F * n + r][h : h + 1] * v_ref[r, m, rows].astype(F32)
                    acc = term if acc is None else acc + term
            acc_ref[i, rows] = acc

    def loop(low, high, blocks, fresh):
        def step(i, carry):
            attend(i, blocks, fresh)
            return carry

        lax.fori_loop(low, high, step, 0)

    backs = [
        remote(done_ref.at[i], back_ref.at[mine], bs_sem.at[i], br_sem.at[mine], (F * team + i, ih))
        for i in range(F)
    ]

    def finish(pair):
        blended = []
        for i in pair:
            scale = 1.0 / l_ref[i]
            blended.append(
                jnp.concatenate(
                    [
                        (acc_ref[i, pl.ds(HEAD_DIM * h, HEAD_DIM)] * scale[h : h + 1]).astype(BF16)
                        for h in range(HEADS)
                    ],
                    axis=0,
                )
            )
        mixed = product(wo_ref[...], jnp.concatenate(blended, axis=1))
        for n, i in enumerate(pair):
            done_ref[i] = (stream_ref[i].astype(F32) + mixed[:, LANES * n : LANES * (n + 1)]).astype(BF16)
        for i in pair:

            @pl.when(mine != i)
            def _():
                backs[i].start()

            @pl.when(mine == i)
            def _():
                back_ref[mine] = done_ref[i]

    def own_keys(members):
        low, high = members[0], members[-1]
        if low == 0:
            left = edge_frame(1, team > 0, 0)
        else:
            left = roll(silu(near_ref[1 + low].astype(F32)), WIDE)
        if high == F - 1:
            right = edge_frame(2, team < teams - 1, F - 1)
        else:
            right = roll(silu(near_ref[3 + high].astype(F32)), -WIDE)
        count = len(members)
        streams, normed, first_frame = temporal(
            [near_ref[2 + i].astype(F32) for i in members],
            [left] + [None] * (count - 1),
            [None] * (count - 1) + [right],
        )
        if low == 0:
            rim_ref[...] = first_frame
        made = product(wqkv_ref[...], normed)
        for n, i in enumerate(members):
            stream_ref[i] = streams[n]
            part = made[:, LANES * n : LANES * (n + 1)]
            query, value = part[:C].astype(BF16), part[2 * C :].astype(BF16)
            for r in range(F):
                q_ref[r, i] = roll(query, WIDE * r)
                v_ref[r, 2 + i] = roll(value, -WIDE * r)
            k_ref[2 + i] = part[C : 2 * C].astype(BF16)

    @pl.when(team < teams - 1)
    def _():
        edge_arrived(2)

    @pl.when(jnp.logical_not(first))
    def _():
        @pl.when(team > 0)
        def _():
            edge_arrived(1)

        own_keys((0, 1, 2, 3))
        loop(0, F, (2, 3, 4, 5), True)

    @pl.when(first)
    def _():
        own_keys((1, 2, 3))
        open_earlier()
        for m in (0, 1):
            remote(
                near_ref.at[2 + m],
                near_ref.at[6 + m],
                zs_sem.at[m],
                zr_sem.at[6 + m],
                (F * earlier + mine, ih),
            ).start()

        loop(1, F, (3, 4, 5), True)

        @pl.when(team < teams - 1)
        def _():
            next_keys()

        edge_arrived(1)
        own_keys((0,))
        attend(0, (2, 3, 4), True)
        attend(1, (2,), False)
        attend(2, (2,), False)


    def side(places, pair):
        for i in pair:
            attend(i, places, False)
        finish(pair)

    @pl.when(team == 0)
    def _():
        finish((0, 1))

    @pl.when((team < teams - 1) & jnp.logical_not(first))
    def _():
        next_keys()

    @pl.when(team < teams - 1)
    def _():
        side((6, 7), (2, 3))

    @pl.when(team == teams - 1)
    def _():
        finish((2, 3))

    @pl.when(team > 0)
    def _():
        side_keys(
            (0, 1),
            0,
            lambda: [edge_frame(0, True, 0), None],
            lambda: [None, rim_ref[...]],
        )
        side((0, 1), (0, 1))

    for step in (1, 3, 2):
        member = lax.rem(mine + step, F)
        remote(
            done_ref.at[0],
            back_ref.at[member],
            bs_sem.at[0],
            br_sem.at[member],
            (it, h_next),
        ).wait_recv()
    lines = [back_ref[j].astype(F32) for j in range(F)]
    for f in range(F):
        whole = lines[0] if f == 0 else roll(lines[0], -WIDE * f)
        for j in range(1, F):
            whole = jnp.where(group == j, roll(lines[j], WIDE * (j - f)), whole)
        out_ref[f] = whole.astype(BF16)

    @pl.when(ih < nh - 1)
    def _():
        row_down.wait_send()

    @pl.when(ih > 0)
    def _():
        row_up.wait_send()

    for j in range(F):

        @pl.when(mine != j)
        def _():
            swaps[j].wait_send()

        @pl.when(mine != j)
        def _():
            backs[j].wait_send()

        @pl.when(edge_wanted)
        def _():
            edges[j].wait_send()

    for j in (0, F - 1):

        @pl.when(direct & (mine >= 2))
        def _():
            straight[j].wait_send()

    for sent, copy in halos:

        @pl.when(sent)
        def _():
            copy.wait_send()


def per_device(
    frames_in, conv_spatial, conv_temporal, w_query, w_key, w_value, w_out, win_left, win_right
):
    hbm = pl.BlockSpec(memory_space=pltpu.HBM)
    frame = (C, LANES)
    return pl.pallas_call(
        kernel,
        out_shape=jax.ShapeDtypeStruct(frames_in.shape, BF16),
        in_specs=[hbm] * 9,
        out_specs=pl.BlockSpec(memory_space=pltpu.VMEM),
        scratch_shapes=[
            pltpu.VMEM((F,) + frame, BF16),
            pltpu.VMEM((C, 9 * C), BF16),
            pltpu.VMEM((C, 3 * C), BF16),
            pltpu.VMEM((3 * C, C), BF16),
            pltpu.VMEM((C, C), BF16),
            pltpu.SMEM((HEADS,), jnp.int32),
            pltpu.SMEM((HEADS,), jnp.int32),
            pltpu.VMEM((F,) + frame, F32),
            pltpu.VMEM((F + 2, 3 * C, LANES), BF16),
            pltpu.VMEM((2,) + frame, BF16),
            pltpu.VMEM((F,) + frame, BF16),
            pltpu.VMEM((F, QUARTER, LANES), BF16),
            pltpu.VMEM((2 * F,) + frame, BF16),
            pltpu.VMEM((F, QUARTER, LANES), BF16),
            pltpu.VMEM((F, 3 * C, LANES), BF16),
            pltpu.VMEM((F,) + frame, BF16),
            pltpu.VMEM((F,) + frame, BF16),
            pltpu.VMEM((F,) + frame, BF16),
            pltpu.VMEM(frame, F32),
            pltpu.VMEM((F, F) + frame, BF16),
            pltpu.VMEM((2 * F,) + frame, BF16),
            pltpu.VMEM((F, 2 * F) + frame, BF16),
            pltpu.VMEM((F,) + frame, F32),
            pltpu.VMEM((F, 8, LANES), F32),
            pltpu.VMEM((F, 8, LANES), F32),
            pltpu.SemaphoreType.DMA((9,)),
            pltpu.SemaphoreType.DMA((2,)),
            pltpu.SemaphoreType.DMA((2,)),
            pltpu.SemaphoreType.DMA((F,)),
            pltpu.SemaphoreType.DMA((F,)),
            pltpu.SemaphoreType.DMA((F,)),
            pltpu.SemaphoreType.DMA((F,)),
            pltpu.SemaphoreType.DMA((F,)),
            pltpu.SemaphoreType.DMA((2 * F,)),
            pltpu.SemaphoreType.DMA((F,)),
            pltpu.SemaphoreType.DMA((F,)),
            pltpu.SemaphoreType.DMA((F,)),
            pltpu.SemaphoreType.REGULAR,
        ],
        compiler_params=pltpu.CompilerParams(
            collective_id=0, has_side_effects=True, vmem_limit_bytes=40 * 1024 * 1024
        ),
    )(
        *(
            pltpu.with_memory_space_constraint(v, pltpu.HBM)
            for v in (
                win_left,
                win_right,
                frames_in,
                conv_spatial,
                conv_temporal,
                w_query,
                w_key,
                w_value,
                w_out,
            )
        )
    )


def solution(mesh):
    return jax.shard_map(
        per_device,
        mesh=mesh,
        in_specs=(P("tm", None, "height"), P(), P(), P(), P(), P(), P(), P(), P()),
        out_specs=P("tm", None, "height"),
        check_vma=False,
    )
```

```python
import functools

import jax
import jax.numpy as jnp
from jax import lax
from jax.experimental import pallas as pl
from jax.experimental.pallas import tpu as pltpu
from jax.sharding import PartitionSpec as P

HEADS = 5
HEAD_DIM = 64
WIDE = 32
C = 320
F = 4
LANES = 128
QUARTER = C // F
COLUMN = 16
MESH = pl.DeviceIdType.MESH
F32 = jnp.float32
BF16 = jnp.bfloat16


def silu(v):
    return 0.5 * v * (1.0 + jnp.tanh(0.5 * v))


def roll(v, shift):
    shift = shift % LANES
    return v if shift == 0 else pltpu.roll(v, shift, 1)


def kernel(
    wl_hbm,
    wr_hbm,
    x_hbm,
    cs_hbm,
    ct_hbm,
    wq_hbm,
    wk_hbm,
    wv_hbm,
    wo_hbm,
    out_ref,
    x_ref,
    cs_ref,
    ct_ref,
    wqkv_ref,
    wo_ref,
    wl_ref,
    wr_ref,
    rows_ref,
    taps_ref,
    above_ref,
    settled_ref,
    edge_ref,
    near_ref,
    far_ref,
    steps_ref,
    stream_ref,
    done_ref,
    back_ref,
    rim_ref,
    q_ref,
    k_ref,
    v_ref,
    acc_ref,
    m_ref,
    l_ref,
    load_sem,
    hs_sem,
    hr_sem,
    gs_sem,
    gr_sem,
    es_sem,
    er_sem,
    zs_sem,
    zr_sem,
    bs_sem,
    br_sem,
    ds_sem,
    ok_sem,
):
    nt = lax.axis_size("tm")
    nh = lax.axis_size("height")
    it = lax.axis_index("tm")
    ih = lax.axis_index("height")
    h_next, h_prev = lax.rem(ih + 1, nh), lax.rem(ih + nh - 1, nh)
    team, mine, teams = it // F, lax.rem(it, F), nt // F
    odd = lax.rem(mine, 2)
    later, earlier = lax.rem(team + 1, teams), lax.rem(team + teams - 1, teams)

    loads = []
    for n, (src, dst) in enumerate(
        (
            (x_hbm, x_ref),
            (cs_hbm, cs_ref),
            (ct_hbm, ct_ref),
            (wq_hbm, wqkv_ref.at[pl.ds(0, C)]),
            (wk_hbm, wqkv_ref.at[pl.ds(C, C)]),
            (wv_hbm, wqkv_ref.at[pl.ds(2 * C, C)]),
            (wo_hbm, wo_ref),
            (wl_hbm, wl_ref),
            (wr_hbm, wr_ref),
        )
    ):
        copy = pltpu.make_async_copy(src, dst, load_sem.at[n])
        copy.start()
        loads.append(copy)

    barrier = pltpu.get_barrier_semaphore()
    friends = [(it, h_next), (it, h_prev)]
    friends += [(F * team + lax.rem(mine + step, F), ih) for step in (1, 2, 3)]
    for dev in friends:
        pl.semaphore_signal(barrier, inc=1, device_id=dev, device_id_type=MESH)

    @pl.when(team > 0)
    def _():
        for j in range(F):
            pl.semaphore_signal(barrier, inc=1, device_id=(F * earlier + j, ih), device_id_type=MESH)

    greetings = len(friends) + F * jnp.where(team < teams - 1, 1, 0)

    def remote(src, dst, ssem, rsem, dev):
        return pltpu.make_async_remote_copy(
            src_ref=src, dst_ref=dst, send_sem=ssem, recv_sem=rsem, device_id=dev, device_id_type=MESH
        )

    lane = lax.broadcasted_iota(jnp.int32, (C, LANES), 1)
    col = jnp.bitwise_and(lane, WIDE - 1)
    group = lax.shift_right_logical(lane, 5)
    block_group = lax.shift_right_logical(lax.broadcasted_iota(jnp.int32, (QUARTER, LANES), 1), 5)

    def fill(place, act):
        taps_ref[place, pl.ds(0, C)] = jnp.where(col == 0, 0.0, roll(act, 1)).astype(BF16)
        taps_ref[place, pl.ds(C, C)] = act.astype(BF16)
        taps_ref[place, pl.ds(2 * C, C)] = jnp.where(col == WIDE - 1, 0.0, roll(act, -1)).astype(BF16)

    loads[0].wait()
    frames = [x_ref[f].astype(F32) for f in range(F)]
    for j in range(F):
        row = jnp.zeros((C, LANES), F32)
        for f in range(F):
            row = jnp.where(group == f, roll(frames[f], WIDE * (f - j)), row)
        rows_ref[j] = row
        fill(j + 1, silu(row))

    pl.semaphore_wait(barrier, greetings)
    first = (team > 0) & (lax.rem(team, COLUMN) == 0)
    direct = (team < teams - 1) & (lax.rem(team, COLUMN) == COLUMN - 1)
    outer_row = jnp.where(mine == 0, 1, 0)
    straight = {}
    row_down = remote(
        taps_ref.at[F, pl.ds(C, C)], above_ref.at[0], hs_sem.at[0], hr_sem.at[0], (it, h_next)
    )
    row_up = remote(
        taps_ref.at[1, pl.ds(C, C)], above_ref.at[1], hs_sem.at[1], hr_sem.at[1], (it, h_prev)
    )

    @pl.when(ih < nh - 1)
    def _():
        row_down.start()

    @pl.when(ih > 0)
    def _():
        row_up.start()

    @pl.when(team < teams - 1)
    def _():
        for j in range(F):
            pl.semaphore_signal(ok_sem, inc=1, device_id=(F * later + j, ih), device_id_type=MESH)


    def around(j):
        return taps_ref[pl.ds(j, 3)].reshape(9 * C, LANES)

    def product(weights, source):
        return jnp.dot(weights, source, preferred_element_type=F32)

    swaps, edges = {}, {}
    edge_team = jnp.where(odd == 1, later, earlier)
    edge_slot = jnp.where(odd == 1, 0, 2) + mine // 2
    edge_wanted = jnp.where(odd == 1, jnp.where(team < teams - 1, 1, 0), jnp.where(team > 0, 1, 0)) == 1

    def settle(j, spatial):
        settled = (rows_ref[j] + spatial).astype(BF16)
        settled_ref[j] = settled
        wide = settled.astype(F32)
        block = jnp.zeros((QUARTER, LANES), F32)
        for n in range(F):
            part = wide[QUARTER * n : QUARTER * (n + 1)]
            turned = jnp.where(odd == 1, roll(part, WIDE * (n + 1)), roll(part, WIDE * n))
            block = jnp.where(block_group == n, turned, block)
        edge_ref[j] = block.astype(BF16)
        edges[j] = remote(
            edge_ref.at[j], far_ref.at[edge_slot], es_sem.at[j], er_sem.at[edge_slot], (F * edge_team + j, ih)
        )

        @pl.when((odd == 1) & (team < teams - 1))
        def _():
            edges[j].start()

        swaps[j] = remote(
            settled_ref.at[j], near_ref.at[2 + mine], gs_sem.at[j], gr_sem.at[mine], (F * team + j, ih)
        )

        if j == 0:
            place = jnp.maximum(mine - 2, 0)
            straight[j] = remote(
                settled_ref.at[j], near_ref.at[place], ds_sem.at[j], zr_sem.at[place], (F * later + j, ih)
            )

            @pl.when(direct & (mine >= 2))
            def _():
                straight[j].start()

        @pl.when(mine != j)
        def _():
            swaps[j].start()

        @pl.when(mine == j)
        def _():
            near_ref[2 + j] = settled

    loads[1].wait()
    inner = product(cs_ref[...], jnp.concatenate([around(1), around(2)], axis=1))
    settle(1, inner[:, :LANES])
    settle(2, inner[:, LANES:])
    middle = product(
        cs_ref[:, 1024:1920],
        jnp.concatenate([taps_ref[1, pl.ds(64, 896)], taps_ref[F, pl.ds(64, 896)]], axis=1),
    )

    @pl.when(ih > 0)
    def _():
        row_down.wait_recv()

    @pl.when(ih < nh - 1)
    def _():
        row_up.wait_recv()

    fill(0, jnp.where(ih > 0, above_ref[0].astype(F32), 0.0))
    fill(F + 1, jnp.where(ih < nh - 1, above_ref[1].astype(F32), 0.0))
    outer = product(
        cs_ref[:, 0:1024], jnp.concatenate([around(0)[0:1024], around(3)[0:1024]], axis=1)
    )
    outer += product(
        cs_ref[:, 1920:2880], jnp.concatenate([taps_ref[2], taps_ref[F + 1]], axis=1)
    )
    outer += middle
    settle(0, outer[:, :LANES])
    settle(3, outer[:, LANES:])

    def open_earlier():
        pl.semaphore_wait(ok_sem, F)

        @pl.when(odd == 0)
        def _():
            for j in range(F):
                edges[j].start()

    @pl.when((team > 0) & jnp.logical_not(first))
    def _():
        open_earlier()

    def swapped(member):
        return remote(
            settled_ref.at[0], near_ref.at[2 + member], gs_sem.at[0], gr_sem.at[member], (it, h_next)
        )

    def wanted(late):
        return jnp.where(late, jnp.where(team < teams - 1, 1, 0), jnp.where(team > 0, 1, 0)) == 1

    halos = []

    def send_halo(member):
        late = member >= 2
        place = jnp.where(late, member - 2, member + 6)
        copy = remote(
            near_ref.at[2 + member],
            near_ref.at[place],
            zs_sem.at[member],
            zr_sem.at[place],
            (F * jnp.where(late, later, earlier) + mine, ih),
        )
        sent = wanted(late) & jnp.logical_not(late & direct & (outer_row == 1))
        halos.append((sent, copy))

        @pl.when(sent & (late | jnp.logical_not(first)))
        def _():
            copy.start()

    send_halo(mine)
    for n in (2, 3, 4, 5, 6, 7, 8):
        loads[n].wait()
    for step in (1, 3, 2):
        member = lax.rem(mine + step, F)
        swapped(member).wait_recv()
        send_halo(member)

    def edge_arrived(slot):
        remote(edge_ref.at[0], far_ref.at[slot], es_sem.at[0], er_sem.at[slot], (it, h_next)).wait_recv()

    def halo_arrived(place):
        remote(near_ref.at[2], near_ref.at[place], zs_sem.at[0], zr_sem.at[place], (it, h_next)).wait_recv()

    def edge_frame(slot, there, place):
        block = silu(jnp.where(there, far_ref[slot].astype(F32), 0.0))
        return jnp.concatenate([roll(block, WIDE * (place - n)) for n in range(F)], axis=0)

    def temporal(values, lefts, rights):
        count = len(values)
        ahead, behind = [], []
        for m in range(count):
            moving = silu(values[m])
            steps_ref[m, pl.ds(C, C)] = moving.astype(BF16)
            ahead.append(roll(moving, WIDE))
            behind.append(roll(moving, -WIDE))
        for m in range(count):
            left = ahead[m - 1] if lefts[m] is None else lefts[m]
            right = behind[m + 1] if rights[m] is None else rights[m]
            steps_ref[m, pl.ds(0, C)] = jnp.where(group == 0, left, ahead[m]).astype(BF16)
            steps_ref[m, pl.ds(2 * C, C)] = jnp.where(group == F - 1, right, behind[m]).astype(BF16)
        total = product(ct_ref[...], jnp.concatenate([steps_ref[m] for m in range(count)], axis=1))
        streams, normed = [], []
        for m in range(count):
            stream = (values[m] + total[:, LANES * m : LANES * (m + 1)]).astype(BF16)
            wide = stream.astype(F32)
            centred = wide - jnp.sum(wide, axis=0, keepdims=True) * (1.0 / C)
            spread = jnp.sum(centred * centred, axis=0, keepdims=True) * (1.0 / C)
            streams.append(stream)
            normed.append((centred * lax.rsqrt(spread + 1e-05)).astype(BF16))
        return streams, jnp.concatenate(normed, axis=1), behind[0]

    def side_keys(places, edge, lefts, rights):
        edge_arrived(edge)
        for place in places:
            halo_arrived(place)
        normed = temporal([near_ref[place].astype(F32) for place in places], lefts(), rights())[1]
        made = product(wqkv_ref[pl.ds(C, 2 * C)], normed)
        for n, place in enumerate(places):
            part = made[:, LANES * n : LANES * (n + 1)].astype(BF16)
            k_ref[place] = part[:C]
            for r in range(F):
                v_ref[r, place] = roll(part[C:], -WIDE * r)

    def next_keys():
        side_keys(
            (6, 7),
            3,
            lambda: [roll(silu(near_ref[5].astype(F32)), WIDE), None],
            lambda: [None, edge_frame(3, True, F - 1)],
        )

    head_row = lax.broadcasted_iota(jnp.int32, (8, LANES), 0)
    lane_frame = lax.shift_right_logical(lax.broadcasted_iota(jnp.int32, (8, LANES), 1), 5)
    reach_left = jnp.zeros((8, LANES), jnp.int32)
    reach_right = jnp.zeros((8, LANES), jnp.int32)
    for h in range(HEADS):
        reach_left = jnp.where(head_row == h, wl_ref[h], reach_left)
        reach_right = jnp.where(head_row == h, wr_ref[h], reach_right)
    summing = jnp.where(
        lax.shift_right_logical(lax.broadcasted_iota(jnp.int32, (16, C), 1), 6)
        == lax.broadcasted_iota(jnp.int32, (16, C), 0),
        1.0,
        0.0,
    ).astype(BF16)

    def attend(i, blocks, fresh):
        masked = []
        for m in blocks:
            products = jnp.concatenate([q_ref[r, i] * k_ref[m] for r in range(F)], axis=1)
            scores = product(summing, products)[:8] * HEAD_DIM ** (-0.5)
            for r in range(F):
                turned = roll(scores[:, LANES * r : LANES * (r + 1)], -WIDE * r)
                offset = F * (m - 2 - i) + jnp.bitwise_and(lane_frame + r, F - 1) - lane_frame
                allowed = (offset >= -reach_left) & (offset <= reach_right)
                masked.append(jnp.where(allowed, turned, -1e30))
        highest = functools.reduce(jnp.maximum, masked)
        if not fresh:
            before = m_ref[i]
            highest = jnp.maximum(highest, before)
            fade = jnp.exp(before - highest)
        raised = [jnp.exp(one - highest) for one in masked]
        total = functools.reduce(jnp.add, raised)
        if not fresh:
            total = total + l_ref[i] * fade
        m_ref[i] = highest
        l_ref[i] = total
        for h in range(HEADS):
            rows = pl.ds(HEAD_DIM * h, HEAD_DIM)
            acc = None if fresh else acc_ref[i, rows] * fade[h : h + 1]
            for n, m in enumerate(blocks):
                for r in range(F):
                    term = raised[F * n + r][h : h + 1] * v_ref[r, m, rows].astype(F32)
                    acc = term if acc is None else acc + term
            acc_ref[i, rows] = acc

    def loop(low, high, blocks, fresh):
        def step(i, carry):
            attend(i, blocks, fresh)
            return carry

        lax.fori_loop(low, high, step, 0)

    backs = [
        remote(done_ref.at[i], back_ref.at[mine], bs_sem.at[i], br_sem.at[mine], (F * team + i, ih))
        for i in range(F)
    ]

    def finish(pair):
        blended = []
        for i in pair:
            scale = 1.0 / l_ref[i]
            blended.append(
                jnp.concatenate(
                    [
                        (acc_ref[i, pl.ds(HEAD_DIM * h, HEAD_DIM)] * scale[h : h + 1]).astype(BF16)
                        for h in range(HEADS)
                    ],
                    axis=0,
                )
            )
        mixed = product(wo_ref[...], jnp.concatenate(blended, axis=1))
        for n, i in enumerate(pair):
            done_ref[i] = (stream_ref[i].astype(F32) + mixed[:, LANES * n : LANES * (n + 1)]).astype(BF16)
        for i in pair:

            @pl.when(mine != i)
            def _():
                backs[i].start()

            @pl.when(mine == i)
            def _():
                back_ref[mine] = done_ref[i]

    def own_keys(members):
        low, high = members[0], members[-1]
        if low == 0:
            left = edge_frame(1, team > 0, 0)
        else:
            left = roll(silu(near_ref[1 + low].astype(F32)), WIDE)
        if high == F - 1:
            right = edge_frame(2, team < teams - 1, F - 1)
        else:
            right = roll(silu(near_ref[3 + high].astype(F32)), -WIDE)
        count = len(members)
        streams, normed, first_frame = temporal(
            [near_ref[2 + i].astype(F32) for i in members],
            [left] + [None] * (count - 1),
            [None] * (count - 1) + [right],
        )
        if low == 0:
            rim_ref[...] = first_frame
        made = product(wqkv_ref[...], normed)
        for n, i in enumerate(members):
            stream_ref[i] = streams[n]
            part = made[:, LANES * n : LANES * (n + 1)]
            query, value = part[:C].astype(BF16), part[2 * C :].astype(BF16)
            for r in range(F):
                q_ref[r, i] = roll(query, WIDE * r)
                v_ref[r, 2 + i] = roll(value, -WIDE * r)
            k_ref[2 + i] = part[C : 2 * C].astype(BF16)

    @pl.when(team < teams - 1)
    def _():
        edge_arrived(2)

    @pl.when(jnp.logical_not(first))
    def _():
        @pl.when(team > 0)
        def _():
            edge_arrived(1)

        own_keys((0, 1, 2, 3))
        loop(0, F, (2, 3, 4, 5), True)

    @pl.when(first)
    def _():
        own_keys((1, 2, 3))
        open_earlier()
        for m in (0, 1):
            remote(
                near_ref.at[2 + m],
                near_ref.at[6 + m],
                zs_sem.at[m],
                zr_sem.at[6 + m],
                (F * earlier + mine, ih),
            ).start()

        loop(1, F, (3, 4, 5), True)

        @pl.when(team < teams - 1)
        def _():
            next_keys()

        edge_arrived(1)
        own_keys((0,))
        attend(0, (2, 3, 4), True)
        attend(1, (2,), False)
        attend(2, (2,), False)


    def side(places, pair):
        for i in pair:
            attend(i, places, False)
        finish(pair)

    @pl.when(team == 0)
    def _():
        finish((0, 1))

    @pl.when((team < teams - 1) & jnp.logical_not(first))
    def _():
        next_keys()

    @pl.when(team < teams - 1)
    def _():
        side((6, 7), (2, 3))

    @pl.when(team == teams - 1)
    def _():
        finish((2, 3))

    @pl.when(team > 0)
    def _():
        side_keys(
            (0, 1),
            0,
            lambda: [edge_frame(0, True, 0), None],
            lambda: [None, rim_ref[...]],
        )
        side((0, 1), (0, 1))

    for step in (1, 3, 2):
        member = lax.rem(mine + step, F)
        remote(
            done_ref.at[0],
            back_ref.at[member],
            bs_sem.at[0],
            br_sem.at[member],
            (it, h_next),
        ).wait_recv()
    lines = [back_ref[j].astype(F32) for j in range(F)]
    for f in range(F):
        whole = lines[0] if f == 0 else roll(lines[0], -WIDE * f)
        for j in range(1, F):
            whole = jnp.where(group == j, roll(lines[j], WIDE * (j - f)), whole)
        out_ref[f] = whole.astype(BF16)

    @pl.when(ih < nh - 1)
    def _():
        row_down.wait_send()

    @pl.when(ih > 0)
    def _():
        row_up.wait_send()

    for j in range(F):

        @pl.when(mine != j)
        def _():
            swaps[j].wait_send()

        @pl.when(mine != j)
        def _():
            backs[j].wait_send()

        @pl.when(edge_wanted)
        def _():
            edges[j].wait_send()

    for j in (0,):

        @pl.when(direct & (mine >= 2))
        def _():
            straight[j].wait_send()

    for sent, copy in halos:

        @pl.when(sent)
        def _():
            copy.wait_send()


def per_device(
    frames_in, conv_spatial, conv_temporal, w_query, w_key, w_value, w_out, win_left, win_right
):
    hbm = pl.BlockSpec(memory_space=pltpu.HBM)
    frame = (C, LANES)
    return pl.pallas_call(
        kernel,
        out_shape=jax.ShapeDtypeStruct(frames_in.shape, BF16),
        in_specs=[hbm] * 9,
        out_specs=pl.BlockSpec(memory_space=pltpu.VMEM),
        scratch_shapes=[
            pltpu.VMEM((F,) + frame, BF16),
            pltpu.VMEM((C, 9 * C), BF16),
            pltpu.VMEM((C, 3 * C), BF16),
            pltpu.VMEM((3 * C, C), BF16),
            pltpu.VMEM((C, C), BF16),
            pltpu.SMEM((HEADS,), jnp.int32),
            pltpu.SMEM((HEADS,), jnp.int32),
            pltpu.VMEM((F,) + frame, F32),
            pltpu.VMEM((F + 2, 3 * C, LANES), BF16),
            pltpu.VMEM((2,) + frame, BF16),
            pltpu.VMEM((F,) + frame, BF16),
            pltpu.VMEM((F, QUARTER, LANES), BF16),
            pltpu.VMEM((2 * F,) + frame, BF16),
            pltpu.VMEM((F, QUARTER, LANES), BF16),
            pltpu.VMEM((F, 3 * C, LANES), BF16),
            pltpu.VMEM((F,) + frame, BF16),
            pltpu.VMEM((F,) + frame, BF16),
            pltpu.VMEM((F,) + frame, BF16),
            pltpu.VMEM(frame, F32),
            pltpu.VMEM((F, F) + frame, BF16),
            pltpu.VMEM((2 * F,) + frame, BF16),
            pltpu.VMEM((F, 2 * F) + frame, BF16),
            pltpu.VMEM((F,) + frame, F32),
            pltpu.VMEM((F, 8, LANES), F32),
            pltpu.VMEM((F, 8, LANES), F32),
            pltpu.SemaphoreType.DMA((9,)),
            pltpu.SemaphoreType.DMA((2,)),
            pltpu.SemaphoreType.DMA((2,)),
            pltpu.SemaphoreType.DMA((F,)),
            pltpu.SemaphoreType.DMA((F,)),
            pltpu.SemaphoreType.DMA((F,)),
            pltpu.SemaphoreType.DMA((F,)),
            pltpu.SemaphoreType.DMA((F,)),
            pltpu.SemaphoreType.DMA((2 * F,)),
            pltpu.SemaphoreType.DMA((F,)),
            pltpu.SemaphoreType.DMA((F,)),
            pltpu.SemaphoreType.DMA((F,)),
            pltpu.SemaphoreType.REGULAR,
        ],
        compiler_params=pltpu.CompilerParams(
            collective_id=0, has_side_effects=True, vmem_limit_bytes=40 * 1024 * 1024
        ),
    )(
        *(
            pltpu.with_memory_space_constraint(v, pltpu.HBM)
            for v in (
                win_left,
                win_right,
                frames_in,
                conv_spatial,
                conv_temporal,
                w_query,
                w_key,
                w_value,
                w_out,
            )
        )
    )


def solution(mesh):
    return jax.shard_map(
        per_device,
        mesh=mesh,
        in_specs=(P("tm", None, "height"), P(), P(), P(), P(), P(), P(), P(), P()),
        out_specs=P("tm", None, "height"),
        check_vma=False,
    )
```
